512 devices in a mesh: row: 32 (over x, z_lo), col: 16 (over y, z_hi, core).
Axes of the slice: x: 4, y: 4, z: 16 (z_hi: 2, z_lo: 8; z = z_hi * 8 + z_lo), core: 2. Of those that a mesh axis runs over, the one named last changes fastest.
Arguments:
- z_iter: float32 [8192, 8192], P('col', 'row'), may hold values from -6 to 6
- y_iter: float32 [8192, 8192], P('col', 'row'), may hold values from -6 to 6
Outputs:
- z_next: float32 [8192, 8192], P('col', 'row')
The draws below stay inside these ranges and needn't reach their ends.
All inputs are finite; a program needn't handle non-finite values.
Results may differ from the reference program's by a relative error of at most 0.0041.
Values may be sent and summed in bfloat16 or wider, within the bound.
No kernel may reach another device: no remote copies, remote signals or barrier semaphores. Data moves between devices by JAX's collectives and lax.ppermute only.
A program may use at most 64 MiB of HBM per device.

```python
import jax
import jax.numpy as jnp

MEMBERS = 8192


def block_scale(rng, dims, pieces, least, largest):
    level = 1.0
    for dim, parts in pieces:
        draws = jax.random.uniform(jax.random.fold_in(jax.random.fold_in(rng, 6), dim), (parts,), jnp.float32, least / len(pieces), largest / len(pieces))
        level = level * jnp.repeat(jnp.exp(draws), dims[dim] // parts).reshape((-1,) + (1,) * (len(dims) - 1 - dim))
    return level


def scatter_about(rng, extent, scale, most, shards=(), kind=jnp.bfloat16):
    values = jax.random.normal(rng, extent, jnp.float32) * scale
    if len(shards) > 0:
        values = block_scale(rng, extent, shards, -0.22, 0.18) * values
    return jnp.clip(values, min=-most, max=most).astype(kind)


def setup_inputs(seed: int = 0) -> dict:
    splits = jax.random.split(jax.random.key(seed), 3)
    z_iter = scatter_about(splits[0], (MEMBERS, MEMBERS), 1.0, 6.0, ((0, 16), (1, 32)), jnp.float32)
    y_iter = scatter_about(splits[1], (MEMBERS, MEMBERS), 1.0, 6.0, ((0, 16), (1, 32)), jnp.float32)
    return {"z_iter": z_iter, "y_iter": y_iter}


def reference(z_iter, y_iter):
    z_half = z_iter.astype(jnp.bfloat16)
    y_half = y_iter.astype(jnp.bfloat16)
    product = jnp.dot(z_half, y_half, preferred_element_type=jnp.float32)
    ident = jnp.eye(MEMBERS, dtype=jnp.float32)
    poly = (1.5 * ident - (0.5 / MEMBERS) * product).astype(jnp.bfloat16)
    return jnp.dot(z_half, poly, preferred_element_type=jnp.float32)
```

```python
import jax
import jax.numpy as jnp
from jax import lax
from jax.experimental import pallas as pl
from jax.experimental.pallas import tpu as pltpu
from jax.sharding import Mesh
from jax.sharding import PartitionSpec as P

AXES = ("x", "zl", "y", "zh", "c")
SIZES = (4, 8, 4, 2, 2)
PLANE = ("x", "y")
SWAP = [(0, 1), (1, 0)]


def dot_kernel(z_ref, *refs):
    parts, out_ref = refs[:-1], refs[-1]
    zh = lax.axis_index("zh")
    c = lax.axis_index("c")
    depth = z_ref.shape[2]
    total = None
    for n, part in enumerate(parts):
        first = (zh ^ (n // 2)) * 4 + (c ^ (n % 2)) * 2
        for h in range(2):
            term = jnp.dot(
                z_ref[first + h],
                part[0, h * depth : (h + 1) * depth, :],
                preferred_element_type=jnp.float32,
            )
            total = term if total is None else total + term
    out_ref[0] = total.astype(out_ref.dtype)


def dot_parts(z_rows, parts):
    blocks, rows, cols = z_rows.shape[0], z_rows.shape[1], parts[0].shape[2]
    groups = parts[0].shape[0]
    return pl.pallas_call(
        dot_kernel,
        grid=(groups,),
        in_specs=[pl.BlockSpec(z_rows.shape, lambda j: (0, 0, 0))]
        + [pl.BlockSpec((1,) + p.shape[1:], lambda j: (j, 0, 0)) for p in parts],
        out_specs=pl.BlockSpec((1, rows, cols), lambda j: (j, 0, 0)),
        out_shape=jax.ShapeDtypeStruct((groups, rows, cols), jnp.bfloat16),
        compiler_params=pltpu.CompilerParams(vmem_limit_bytes=32 * 2**20),
        cost_estimate=pl.CostEstimate(
            flops=2 * groups * rows * cols * blocks * z_rows.shape[2],
            bytes_accessed=2 * (z_rows.size + 4 * parts[0].size + groups * rows * cols),
            transcendentals=0,
        ),
    )(z_rows, *parts)


def other_core(block):
    return lax.ppermute(block, "c", SWAP)


def make_shift(product, order):
    groups, rows, cols = product.shape
    at = lambda name: lax.axis_index(name)
    group = lax.broadcasted_iota(jnp.int32, product.shape, 0)
    row_ids = (
        group * 2048
        + at("zh") * 1024
        + at("c") * 512
        + at("y") * rows
        + lax.broadcasted_iota(jnp.int32, product.shape, 1)
    )
    col_ids = at("x") * 2048 + at("zl") * cols + lax.broadcasted_iota(jnp.int32, product.shape, 2)
    ident = jnp.where(row_ids == col_ids, 1.5, 0.0).astype(jnp.float32)
    poly = (ident - 0.5 / order * product).astype(jnp.bfloat16)
    return (poly.astype(jnp.float32) - ident).astype(jnp.bfloat16)


def shards(z_iter, y_iter):
    order = z_iter.shape[1] * lax.axis_size("x") * lax.axis_size("zl")
    z_half = z_iter.astype(jnp.bfloat16)
    y_half = y_iter.astype(jnp.bfloat16)
    z_rows = lax.all_gather(z_half, "zl")

    def y_parts(block):
        every = lax.all_to_all(jnp.stack([block] * 4), "y", 0, 0, tiled=True)
        return [every, other_core(every)]

    turn = [(i * 4 + j, j * 4 + i) for i in range(4) for j in range(4)]
    turned = lax.ppermute(y_half, PLANE, turn)
    swapped = lax.ppermute(turned, "zh", SWAP)
    y_all = y_parts(turned) + y_parts(swapped)

    part = dot_parts(z_rows, y_all)
    part = lax.all_to_all(part.reshape(16, 128, 256), PLANE, 0, 0, tiled=True)
    product = part.reshape(4, 4, 128, 256).astype(jnp.float32).sum(0)
    shift = make_shift(product, order)

    def shift_parts(block):
        spread = jnp.broadcast_to(block[:, None], (4, 4, 128, 256)).reshape(16, 128, 256)
        every = lax.all_to_all(spread, PLANE, 0, 0, tiled=True).reshape(4, 512, 256)
        return [every, other_core(every)]

    shift_all = shift_parts(shift) + shift_parts(lax.ppermute(shift, "zh", SWAP))
    part = dot_parts(z_rows, shift_all)
    part = lax.all_to_all(part, "x", 0, 0, tiled=True)
    return 1.5 * z_half.astype(jnp.float32) + part.astype(jnp.float32).sum(0)


def solution(mesh):
    fine = Mesh(mesh.devices.reshape(SIZES), AXES)
    spec = P(("y", "zh", "c"), ("x", "zl"))
    return jax.shard_map(
        shards,
        mesh=fine,
        in_specs=(spec, spec),
        out_specs=spec,
        check_vma=False,
    )
```

```python
import jax
import jax.numpy as jnp
from jax import lax
from jax.experimental import pallas as pl
from jax.experimental.pallas import tpu as pltpu
from jax.sharding import Mesh
from jax.sharding import PartitionSpec as P

AXES = ("x", "zl", "y", "zh", "c")
SIZES = (4, 8, 4, 2, 2)
PLANE = ("x", "y")
RING = ("zl", "zh")
SWAP = [(0, 1), (1, 0)]


def flat_id(x, zl, y, zh, c):
    return (((x * 8 + zl) * 4 + y) * 2 + zh) * 2 + c


Z_RINGS = [
    [flat_id(x, z % 8, y, z // 8, c) for z in range(16)]
    for x in range(4)
    for y in range(4)
    for c in range(2)
]


def along_z(block, step):
    place = lambda z: (z % 8) * 2 + z // 8
    return lax.ppermute(block, RING, [(place(z), place((z + step) % 16)) for z in range(16)])


def dot_kernel(z_ref, own_ref, other_ref, out_ref, right):
    groups, _, depth, width = own_ref.shape
    c = lax.axis_index("c")

    @pl.when(pl.program_id(0) == 0)
    def _():
        for ref, core in ((own_ref, c), (other_ref, 1 - c)):
            for s in range(4):
                chunk = (s // 2) * 4 + core * 2 + s % 2
                for j in range(groups):
                    right[chunk, :, j * width : (j + 1) * width] = ref[j, s]

    total = jnp.dot(z_ref[0], right[0], preferred_element_type=jnp.float32)
    for k in range(1, 8):
        total += jnp.dot(z_ref[k], right[k], preferred_element_type=jnp.float32)
    for j in range(groups):
        out_ref[j, 0] = total[:, j * width : (j + 1) * width].astype(out_ref.dtype)


def dot_right(z_rows, own, other):
    groups, steps, depth, width = own.shape
    whole = pl.BlockSpec(own.shape, lambda s: (0, 0, 0, 0))
    return pl.pallas_call(
        dot_kernel,
        grid=(steps,),
        in_specs=[pl.BlockSpec((8, depth, depth), lambda s: (s // 2, s % 2, 0)), whole, whole],
        out_specs=pl.BlockSpec((groups, 1, depth, width), lambda s: (0, s, 0, 0)),
        out_shape=jax.ShapeDtypeStruct(own.shape, jnp.bfloat16),
        scratch_shapes=[pltpu.VMEM((8, depth, groups * width), jnp.bfloat16)],
        compiler_params=pltpu.CompilerParams(vmem_limit_bytes=32 * 2**20),
        cost_estimate=pl.CostEstimate(
            flops=2 * z_rows.size * groups * width,
            bytes_accessed=2 * (z_rows.size + 3 * own.size),
            transcendentals=0,
        ),
    )(z_rows, own, other)


def other_core(block):
    return lax.ppermute(block, "c", SWAP)


def make_shift(product, order, first_col):
    at = lax.axis_index
    rows = product.shape[1]
    row_ids = (
        lax.broadcasted_iota(jnp.int32, product.shape, 0) * 2048
        + at("y") // 2 * 1024
        + at("c") * 512
        + at("y") % 2 * rows
        + lax.broadcasted_iota(jnp.int32, product.shape, 1)
    )
    col_ids = first_col + lax.broadcasted_iota(jnp.int32, product.shape, 2)
    ident = jnp.where(row_ids == col_ids, 1.5, 0.0).astype(jnp.float32)
    poly = lax.reduce_precision(ident - 0.5 / order * product, 8, 7)
    return (poly - ident).astype(jnp.bfloat16)


def shards(z_iter, y_iter):
    at = lax.axis_index
    order = z_iter.shape[1] * lax.axis_size("x") * lax.axis_size("zl")
    z_half = z_iter.astype(jnp.bfloat16)
    y_half = y_iter.astype(jnp.bfloat16)
    z_rows = lax.all_gather(z_half, AXES, axis_index_groups=Z_RINGS)

    low = at("zh") == 0
    z = at("zh") * 8 + at("zl")
    middle = (z >= 4) & (z < 12)
    first_col = at("x") * 2048 + (at("zl") ^ 4) * 256 + jnp.where(middle, 0, 128)
    left, right = y_half[:, :128], y_half[:, 128:]
    up = along_z(jnp.where(low, left, right), 4)
    down = along_z(jnp.where(low, right, left), -4)
    y_both = jnp.stack([jnp.where(middle, up, down), jnp.where(middle, down, up)])
    y_both = y_both.reshape(4, 256, 128)

    turn = [(i * 4 + j, j * 4 + i) for i in range(4) for j in range(4)]
    turned = lax.ppermute(y_both, PLANE, turn)
    y_own = lax.all_to_all(jnp.stack([turned] * 4), "y", 0, 0, tiled=True)
    part = dot_right(z_rows, y_own, other_core(y_own))

    part = lax.all_to_all(part.reshape(16, 256, 128), PLANE, 0, 0, tiled=True)
    product = part.reshape(4, 4, 256, 128).astype(jnp.float32).sum(0)
    shift = make_shift(product, order, first_col)

    spread = jnp.broadcast_to(shift[:, None], (4, 4, 256, 128)).reshape(16, 256, 128)
    own = lax.all_to_all(spread, PLANE, 0, 0, tiled=True).reshape(4, 4, 256, 128)
    part = dot_right(z_rows, own, other_core(own))
    part = lax.all_to_all(part, "x", 0, 0, tiled=True)
    part = part.astype(jnp.float32).sum(0).astype(jnp.bfloat16).reshape(2, 512, 128)
    down = along_z(jnp.where(middle, part[0], part[1]), -4)
    up = along_z(jnp.where(middle, part[1], part[0]), 4)
    part = jnp.concatenate([jnp.where(low, down, up), jnp.where(low, up, down)], axis=1)
    return 1.5 * z_half.astype(jnp.float32) + part.astype(jnp.float32)


def solution(mesh):
    fine = Mesh(mesh.devices.reshape(SIZES), AXES)
    spec = P(("y", "zh", "c"), ("x", "zl"))
    return jax.shard_map(
        shards,
        mesh=fine,
        in_specs=(spec, spec),
        out_specs=spec,
        check_vma=False,
    )
```

```python
import jax
import jax.numpy as jnp
from jax import lax
from jax.experimental import pallas as pl
from jax.experimental.pallas import tpu as pltpu
from jax.sharding import Mesh
from jax.sharding import PartitionSpec as P

AXES = ("x", "zl", "y", "zh", "c")
SIZES = (4, 8, 4, 2, 2)
PLANE = ("x", "y")
RING = ("zl", "zh")
SWAP = [(0, 1), (1, 0)]


def along_z(block, step):
    place = lambda z: (z % 8) * 2 + z // 8
    return lax.ppermute(block, RING, [(place(z), place((z + step) % 16)) for z in range(16)])


def round_z(block):
    place = lambda z, c: ((z % 8) * 2 + z // 8) * 2 + c
    pairs = [(place(z, c), place((z + 1 - 2 * c) % 16, c)) for z in range(16) for c in range(2)]
    return lax.ppermute(block, RING + ("c",), pairs)


def dot_kernel(*refs):
    own_ref, other_ref, out_ref, left, right, sem = refs[11:]
    chunks = list(refs[:9]) + [ref.at[n] for ref in refs[9:11] for n in range(ref.shape[0])]
    groups, _, depth, width = own_ref.shape
    c = lax.axis_index("c")
    step = pl.program_id(0)

    @pl.when(step == 0)
    def _():
        z = lax.axis_index("zh") * 8 + lax.axis_index("zl")
        copies = []
        for n, ref in enumerate(chunks):
            away = -n if n <= 8 else n - 8
            at = lax.rem(z + away * (1 - 2 * c) + 16, 16)
            copies.append(pltpu.make_async_copy(ref, left.at[at], sem.at[n]))
        for copy in copies:
            copy.start()
        for ref, core in ((own_ref, c), (other_ref, 1 - c)):
            for s in range(4):
                chunk = (s // 2) * 4 + core * 2 + s % 2
                for j in range(groups):
                    right[chunk, :, j * width : (j + 1) * width] = ref[j, s]
        for copy in copies:
            copy.wait()

    first = (step // 2) * 8
    rows = pl.ds(pl.multiple_of((step % 2) * depth, depth), depth)
    total = jnp.dot(left[first, rows, :], right[0], preferred_element_type=jnp.float32)
    for k in range(1, 8):
        total += jnp.dot(left[first + k, rows, :], right[k], preferred_element_type=jnp.float32)
    for j in range(groups):
        out_ref[j, 0] = total[:, j * width : (j + 1) * width].astype(out_ref.dtype)


def dot_right(z_rows, own, other):
    groups, steps, depth, width = own.shape
    whole = pl.BlockSpec(own.shape, lambda s: (0, 0, 0, 0))
    return pl.pallas_call(
        dot_kernel,
        grid=(steps,),
        in_specs=[pl.BlockSpec(memory_space=pl.ANY)] * 11 + [whole, whole],
        out_specs=pl.BlockSpec((groups, 1, depth, width), lambda s: (0, s, 0, 0)),
        out_shape=jax.ShapeDtypeStruct(own.shape, jnp.bfloat16),
        scratch_shapes=[
            pltpu.VMEM((16,) + z_rows[0].shape, jnp.bfloat16),
            pltpu.VMEM((8, depth, groups * width), jnp.bfloat16),
            pltpu.SemaphoreType.DMA((16,)),
        ],
        compiler_params=pltpu.CompilerParams(vmem_limit_bytes=32 * 2**20),
        cost_estimate=pl.CostEstimate(
            flops=32 * z_rows[0].size * groups * width,
            bytes_accessed=2 * (16 * z_rows[0].size + 3 * own.size),
            transcendentals=0,
        ),
    )(*z_rows, own, other)


def other_core(block):
    return lax.ppermute(block, "c", SWAP)


def make_shift(product, order, first_col):
    at = lax.axis_index
    rows = product.shape[1]
    row_ids = (
        lax.broadcasted_iota(jnp.int32, product.shape, 0) * 2048
        + at("y") // 2 * 1024
        + at("c") * 512
        + at("y") % 2 * rows
        + lax.broadcasted_iota(jnp.int32, product.shape, 1)
    )
    col_ids = first_col + lax.broadcasted_iota(jnp.int32, product.shape, 2)
    ident = jnp.where(row_ids == col_ids, 1.5, 0.0).astype(jnp.float32)
    poly = lax.reduce_precision(ident - 0.5 / order * product, 8, 7)
    return (poly - ident).astype(jnp.bfloat16)


def shards(z_iter, y_iter):
    at = lax.axis_index
    order = z_iter.shape[1] * lax.axis_size("x") * lax.axis_size("zl")
    z_half = z_iter.astype(jnp.bfloat16)
    y_half = y_iter.astype(jnp.bfloat16)

    mine = [round_z(z_half)]
    theirs = [round_z(other_core(z_half))]
    for n in range(1, 8):
        mine.append(round_z(mine[-1]))
        if n < 7:
            theirs.append(round_z(theirs[-1]))
    z_rows = [z_half] + mine
    z_rows += [other_core(jnp.stack(theirs[:4])), other_core(jnp.stack(theirs[4:]))]

    low = at("zh") == 0
    z = at("zh") * 8 + at("zl")
    middle = (z >= 4) & (z < 12)
    first_col = at("x") * 2048 + (at("zl") ^ 4) * 256 + jnp.where(middle, 0, 128)
    left, right = y_half[:, :128], y_half[:, 128:]
    up = along_z(jnp.where(low, left, right), 4)
    down = along_z(jnp.where(low, right, left), -4)
    y_both = jnp.stack([jnp.where(middle, up, down), jnp.where(middle, down, up)])
    y_both = y_both.reshape(4, 256, 128)

    turn = [(i * 4 + j, j * 4 + i) for i in range(4) for j in range(4)]
    turned = lax.ppermute(y_both, PLANE, turn)
    y_own = lax.all_to_all(jnp.stack([turned] * 4), "y", 0, 0, tiled=True)
    part = dot_right(z_rows, y_own, other_core(y_own))

    part = lax.all_to_all(part.reshape(16, 256, 128), PLANE, 0, 0, tiled=True)
    product = part.reshape(4, 4, 256, 128).astype(jnp.float32).sum(0)
    shift = make_shift(product, order, first_col)

    spread = jnp.broadcast_to(shift[:, None], (4, 4, 256, 128)).reshape(16, 256, 128)
    own = lax.all_to_all(spread, PLANE, 0, 0, tiled=True).reshape(4, 4, 256, 128)
    part = dot_right(z_rows, own, other_core(own))
    part = lax.all_to_all(part, "x", 0, 0, tiled=True)
    part = part.astype(jnp.float32).sum(0).astype(jnp.bfloat16).reshape(2, 512, 128)
    down = along_z(jnp.where(middle, part[0], part[1]), -4)
    up = along_z(jnp.where(middle, part[1], part[0]), 4)
    part = jnp.concatenate([jnp.where(low, down, up), jnp.where(low, up, down)], axis=1)
    return 1.5 * z_half.astype(jnp.float32) + part.astype(jnp.float32)


def solution(mesh):
    fine = Mesh(mesh.devices.reshape(SIZES), AXES)
    spec = P(("y", "zh", "c"), ("x", "zl"))
    return jax.shard_map(
        shards,
        mesh=fine,
        in_specs=(spec, spec),
        out_specs=spec,
        check_vma=False,
    )
```

```python
import jax
import jax.numpy as jnp
from jax import lax
from jax.experimental import pallas as pl
from jax.experimental.pallas import tpu as pltpu
from jax.sharding import Mesh
from jax.sharding import PartitionSpec as P

AXES = ("x", "zl", "y", "zh", "c")
SIZES = (4, 8, 4, 2, 2)
PLANE = ("x", "y")
RING = ("zl", "zh")
SWAP = [(0, 1), (1, 0)]


def along_z(block, step):
    place = lambda z: (z % 8) * 2 + z // 8
    return lax.ppermute(block, RING, [(place(z), place((z + step) % 16)) for z in range(16)])


def turn_and_along_z(block, step):
    place = lambda x, z, y: ((x * 8 + z % 8) * 4 + y) * 2 + z // 8
    pairs = [
        (place(x, z, y), place(y, (z + step) % 16, x))
        for x in range(4)
        for y in range(4)
        for z in range(16)
    ]
    return lax.ppermute(block, ("x", "zl", "y", "zh"), pairs)


def dot_kernel(*refs):
    chunks, (own_ref, other_ref, out_ref, left, right, sem) = refs[:16], refs[16:]
    groups, _, depth, width = own_ref.shape
    c = lax.axis_index("c")
    step = pl.program_id(0)

    @pl.when(step == 0)
    def _():
        z = lax.axis_index("zh") * 8 + lax.axis_index("zl")
        copies = []
        for n, ref in enumerate(chunks):
            away = -n if n <= 8 else n - 8
            at = lax.rem(z + away + 16, 16)
            copies.append(pltpu.make_async_copy(ref, left.at[at], sem.at[n]))
        for copy in copies:
            copy.start()
        for ref, core in ((own_ref, c), (other_ref, 1 - c)):
            for s in range(4):
                chunk = (s // 2) * 4 + core * 2 + s % 2
                for j in range(groups):
                    right[chunk, :, j * width : (j + 1) * width] = ref[j, s]
        for copy in copies:
            copy.wait()

    first = (step // 2) * 8
    rows = pl.ds(pl.multiple_of((step % 2) * depth, depth), depth)
    total = jnp.dot(left[first, rows, :], right[0], preferred_element_type=jnp.float32)
    for k in range(1, 8):
        total += jnp.dot(left[first + k, rows, :], right[k], preferred_element_type=jnp.float32)
    for j in range(groups):
        out_ref[j, 0] = total[:, j * width : (j + 1) * width].astype(out_ref.dtype)


def dot_right(z_rows, own, other):
    groups, steps, depth, width = own.shape
    whole = pl.BlockSpec(own.shape, lambda s: (0, 0, 0, 0))
    return pl.pallas_call(
        dot_kernel,
        grid=(steps,),
        in_specs=[pl.BlockSpec(memory_space=pl.ANY)] * 16 + [whole, whole],
        out_specs=pl.BlockSpec((groups, 1, depth, width), lambda s: (0, s, 0, 0)),
        out_shape=jax.ShapeDtypeStruct(own.shape, jnp.bfloat16),
        scratch_shapes=[
            pltpu.VMEM((16,) + z_rows[0].shape, jnp.bfloat16),
            pltpu.VMEM((8, depth, groups * width), jnp.bfloat16),
            pltpu.SemaphoreType.DMA((16,)),
        ],
        compiler_params=pltpu.CompilerParams(vmem_limit_bytes=32 * 2**20),
        cost_estimate=pl.CostEstimate(
            flops=32 * z_rows[0].size * groups * width,
            bytes_accessed=2 * (16 * z_rows[0].size + 3 * own.size),
            transcendentals=0,
        ),
    )(*z_rows, own, other)


def other_core(block):
    return lax.ppermute(block, "c", SWAP)


def make_shift(product, order, first_col):
    at = lax.axis_index
    rows = product.shape[1]
    row_ids = (
        lax.broadcasted_iota(jnp.int32, product.shape, 0) * 2048
        + at("y") // 2 * 1024
        + at("c") * 512
        + at("y") % 2 * rows
        + lax.broadcasted_iota(jnp.int32, product.shape, 1)
    )
    col_ids = first_col + lax.broadcasted_iota(jnp.int32, product.shape, 2)
    ident = jnp.where(row_ids == col_ids, 1.5, 0.0).astype(jnp.float32)
    poly = lax.reduce_precision(ident - 0.5 / order * product, 8, 7)
    return (poly - ident).astype(jnp.bfloat16)


def shards(z_iter, y_iter):
    at = lax.axis_index
    order = z_iter.shape[1] * lax.axis_size("x") * lax.axis_size("zl")
    z_half = z_iter.astype(jnp.bfloat16)
    y_half = y_iter.astype(jnp.bfloat16)

    low = at("zh") == 0
    z = at("zh") * 8 + at("zl")
    middle = (z >= 4) & (z < 12)
    first_col = at("x") * 2048 + (at("zl") ^ 4) * 256 + jnp.where(middle, 0, 128)
    left, right = y_half[:, :128], y_half[:, 128:]
    send_up, send_down = jnp.where(low, left, right), jnp.where(low, right, left)

    tie = lax.optimization_barrier
    ups, downs = [along_z(z_half, 1)], [along_z(z_half, -1)]
    up = along_z(send_up, 2)
    for n in range(2, 9):
        if n == 2:
            up, ups[-1], downs[-1] = tie((up, ups[-1], downs[-1]))
        if n == 3:
            up, send_down, ups[-1], downs[-1] = tie((up, send_down, ups[-1], downs[-1]))
        if n == 4 or n == 5:
            down, ups[-1], downs[-1] = tie((down, ups[-1], downs[-1]))
        if n == 7:
            y_own, ups[-1], downs[-1] = tie((y_own, ups[-1], downs[-1]))
        ups.append(along_z(ups[-1], 1))
        if n < 8:
            downs.append(along_z(downs[-1], -1))
        if n == 2:
            up = turn_and_along_z(up, 2)
        if n == 3:
            down = along_z(send_down, -2)
        if n == 4:
            down = turn_and_along_z(down, -2)
        if n == 5:
            y_both = jnp.stack([jnp.where(middle, up, down), jnp.where(middle, down, up)])
            y_both = y_both.reshape(4, 256, 128)
            y_own = lax.all_to_all(jnp.stack([y_both] * 4), "y", 0, 0, tiled=True)
        if n == 7:
            y_other = other_core(y_own)
    z_rows = [z_half] + ups + downs
    part = dot_right(z_rows, y_own, y_other)

    part = lax.all_to_all(part.reshape(16, 256, 128), PLANE, 0, 0, tiled=True)
    product = part.reshape(4, 4, 256, 128).astype(jnp.float32).sum(0)
    shift = make_shift(product, order, first_col)

    spread = jnp.broadcast_to(shift[:, None], (4, 4, 256, 128)).reshape(16, 256, 128)
    own = lax.all_to_all(spread, PLANE, 0, 0, tiled=True).reshape(4, 4, 256, 128)
    part = dot_right(z_rows, own, other_core(own))
    part = lax.all_to_all(part, "x", 0, 0, tiled=True)
    part = part.astype(jnp.float32).sum(0).astype(jnp.bfloat16).reshape(2, 512, 128)
    down = along_z(jnp.where(middle, part[0], part[1]), -4)
    up = along_z(jnp.where(middle, part[1], part[0]), 4)
    part = jnp.concatenate([jnp.where(low, down, up), jnp.where(low, up, down)], axis=1)
    return 1.5 * z_half.astype(jnp.float32) + part.astype(jnp.float32)


def solution(mesh):
    fine = Mesh(mesh.devices.reshape(SIZES), AXES)
    spec = P(("y", "zh", "c"), ("x", "zl"))
    return jax.shard_map(
        shards,
        mesh=fine,
        in_specs=(spec, spec),
        out_specs=spec,
        check_vma=False,
    )
```

```python
import functools

import jax
import jax.numpy as jnp
from jax import lax
from jax.experimental import pallas as pl
from jax.experimental.pallas import tpu as pltpu
from jax.sharding import Mesh
from jax.sharding import PartitionSpec as P

AXES = ("x", "zl", "y", "zh", "c")
SIZES = (4, 8, 4, 2, 2)
PLANE = ("x", "y")
SWAP = [(0, 1), (1, 0)]


def flat_id(x, zl, y, zh, c):
    return (((x * 8 + zl) * 4 + y) * 2 + zh) * 2 + c


Z_RINGS = [
    [flat_id(x, z % 8, y, z // 8, c) for z in range(16)]
    for x in range(4)
    for y in range(4)
    for c in range(2)
]


def dot_kernel(flips, z_ref, own_ref, other_ref, out_ref, left, sem):
    groups, _, depth, width = own_ref.shape
    c = lax.axis_index("c")
    firsts = [0, 8] if flips is None else [(lax.axis_index("zh") ^ flips) * 8]
    copies = []
    for b, first in enumerate(firsts):
        for n in range(8):
            chunk = (n % 4) // 2 * 4 + (c ^ (n // 4)) * 2 + n % 2
            copies.append(
                pltpu.make_async_copy(z_ref.at[first + chunk], left.at[b * 8 + n], sem.at[b * 8 + n])
            )
    for copy in copies:
        copy.start()
    for s in range(out_ref.shape[1]):
        b, rows = s // 2, slice(s % 2 * depth, (s % 2 + 1) * depth)
        total = None
        for n in range(8):
            if s % 2 == 0:
                copies[b * 8 + n].wait()
            part = (own_ref, other_ref)[n // 4]
            right = jnp.concatenate([part[j, n % 4] for j in range(groups)], axis=1)
            term = jnp.dot(left[b * 8 + n, rows, :], right, preferred_element_type=jnp.float32)
            total = term if total is None else total + term
        for j in range(groups):
            out_ref[j, s] = total[:, j * width : (j + 1) * width].astype(out_ref.dtype)


def dot_right(flips, z_rows, own, other):
    groups, steps, depth, width = own.shape
    chunks = 16 if flips is None else 8
    steps = chunks // 4
    return pl.pallas_call(
        functools.partial(dot_kernel, flips),
        in_specs=[pl.BlockSpec(memory_space=pl.ANY)] + [pl.BlockSpec(memory_space=pltpu.VMEM)] * 2,
        out_specs=pl.BlockSpec(memory_space=pltpu.VMEM),
        out_shape=jax.ShapeDtypeStruct((groups, steps, depth, width), jnp.bfloat16),
        scratch_shapes=[
            pltpu.VMEM((chunks,) + z_rows.shape[1:], jnp.bfloat16),
            pltpu.SemaphoreType.DMA((chunks,)),
        ],
        compiler_params=pltpu.CompilerParams(vmem_limit_bytes=(56 if flips is None else 32) * 2**20),
        cost_estimate=pl.CostEstimate(
            flops=2 * z_rows.size * groups * width * chunks // 16,
            bytes_accessed=2 * (z_rows.size * chunks // 16 + 3 * own.size),
            transcendentals=0,
        ),
    )(z_rows, own, other)


def other_core(block):
    return lax.ppermute(block, "c", SWAP)


def make_shift(product, order, first_col):
    at = lax.axis_index
    rows = product.shape[1]
    row_ids = (
        lax.broadcasted_iota(jnp.int32, product.shape, 0) * 2048
        + at("y") // 2 * 1024
        + at("c") * 512
        + at("y") % 2 * rows
        + lax.broadcasted_iota(jnp.int32, product.shape, 1)
    )
    col_ids = first_col + lax.broadcasted_iota(jnp.int32, product.shape, 2)
    ident = jnp.where(row_ids == col_ids, 1.5, 0.0).astype(jnp.float32)
    poly = lax.reduce_precision(ident - 0.5 / order * product, 8, 7)
    return (poly - ident).astype(jnp.bfloat16)


def shards(z_iter, y_iter):
    at = lax.axis_index
    order = z_iter.shape[1] * lax.axis_size("x") * lax.axis_size("zl")
    z_half = z_iter.astype(jnp.bfloat16)
    y_half = y_iter.astype(jnp.bfloat16)
    z_rows = lax.all_gather(z_half, AXES, axis_index_groups=Z_RINGS)

    zh = at("zh")
    low = zh == 0
    first_col = at("x") * 2048 + at("zl") * 256 + zh * 128
    left, right = y_half[:, :128], y_half[:, 128:]
    mine = jnp.where(low, left, right)
    yours = lax.ppermute(jnp.where(low, right, left), "zh", SWAP)
    y_both = jnp.stack([jnp.where(low, mine, yours), jnp.where(low, yours, mine)])
    y_both = y_both.reshape(4, 256, 128)

    turn = [(i * 4 + j, j * 4 + i) for i in range(4) for j in range(4)]
    turned = lax.ppermute(y_both, PLANE, turn)
    y_own = lax.all_to_all(jnp.stack([turned] * 4), "y", 0, 0, tiled=True)
    part = dot_right(None, z_rows, y_own, other_core(y_own))

    part = lax.all_to_all(part.reshape(16, 256, 128), PLANE, 0, 0, tiled=True)
    product = part.reshape(4, 4, 256, 128).astype(jnp.float32).sum(0)
    shift = make_shift(product, order, first_col)

    spread = jnp.broadcast_to(shift[:, None], (4, 4, 256, 128)).reshape(16, 256, 128)
    own = lax.all_to_all(spread, PLANE, 0, 0, tiled=True).reshape(4, 4, 256, 128)
    other = other_core(own)

    def result(flips):
        part = dot_right(flips, z_rows, own, other)
        part = lax.all_to_all(part, "x", 0, 0, tiled=True)
        return part.astype(jnp.float32).sum(0).reshape(512, 128)

    yours = lax.ppermute(result(1).astype(jnp.bfloat16), "zh", SWAP).astype(jnp.float32)
    mine = result(0)
    part = jnp.concatenate([jnp.where(low, mine, yours), jnp.where(low, yours, mine)], axis=1)
    return 1.5 * z_half.astype(jnp.float32) + part


def solution(mesh):
    fine = Mesh(mesh.devices.reshape(SIZES), AXES)
    spec = P(("y", "zh", "c"), ("x", "zl"))
    return jax.shard_map(
        shards,
        mesh=fine,
        in_specs=(spec, spec),
        out_specs=spec,
        check_vma=False,
    )
```

```python
import functools

import jax
import jax.numpy as jnp
from jax import lax
from jax.experimental import pallas as pl
from jax.experimental.pallas import tpu as pltpu
from jax.sharding import Mesh
from jax.sharding import PartitionSpec as P

AXES = ("x", "zl", "y", "zh", "c")
SIZES = (4, 8, 4, 2, 2)
PLANE = ("x", "y")
SWAP = [(0, 1), (1, 0)]


def flat_id(x, zl, y, zh, c):
    return (((x * 8 + zl) * 4 + y) * 2 + zh) * 2 + c


Z_RINGS = [
    [flat_id(x, z % 8, y, z // 8, c) for z in range(16)]
    for x in range(4)
    for y in range(4)
    for c in range(2)
]


def dot_kernel(flips, z_ref, own_ref, other_ref, out_ref, left, sem):
    groups, _, depth, width = own_ref.shape
    c = lax.axis_index("c")
    first = (lax.axis_index("zh") ^ flips) * 8
    copies = []
    for n in range(8):
        chunk = (n % 4) // 2 * 4 + (c ^ (n // 4)) * 2 + n % 2
        copies.append(pltpu.make_async_copy(z_ref.at[first + chunk], left.at[n], sem.at[n]))
    for copy in copies:
        copy.start()
    for s in range(2):
        total = None
        for n in range(8):
            if s == 0:
                copies[n].wait()
            part = (own_ref, other_ref)[n // 4]
            right = jnp.concatenate([part[j, n % 4] for j in range(groups)], axis=1)
            rows = left[n, s * depth : (s + 1) * depth, :]
            term = jnp.dot(rows, right, preferred_element_type=jnp.float32)
            total = term if total is None else total + term
        for j in range(groups):
            out_ref[j, s] = total[:, j * width : (j + 1) * width].astype(out_ref.dtype)


def dot_all_kernel(z_ref, own_ref, other_ref, out_ref, right):
    groups, _, depth, width = own_ref.shape
    c = lax.axis_index("c")

    @pl.when(pl.program_id(0) == 0)
    def _():
        for ref, core in ((own_ref, c), (other_ref, 1 - c)):
            for n in range(4):
                for j in range(groups):
                    right[n // 2 * 4 + core * 2 + n % 2, :, j * width : (j + 1) * width] = ref[j, n]

    total = jnp.dot(z_ref[0], right[0], preferred_element_type=jnp.float32)
    for k in range(1, 8):
        total += jnp.dot(z_ref[k], right[k], preferred_element_type=jnp.float32)
    for j in range(groups):
        out_ref[j, 0] = total[:, j * width : (j + 1) * width].astype(out_ref.dtype)


def dot_right_all(z_rows, own, other):
    groups, steps, depth, width = own.shape
    whole = pl.BlockSpec(own.shape, lambda s: (0, 0, 0, 0))
    return pl.pallas_call(
        dot_all_kernel,
        grid=(steps,),
        in_specs=[pl.BlockSpec((8, depth, depth), lambda s: (s // 2, s % 2, 0)), whole, whole],
        out_specs=pl.BlockSpec((groups, 1, depth, width), lambda s: (0, s, 0, 0)),
        out_shape=jax.ShapeDtypeStruct(own.shape, jnp.bfloat16),
        scratch_shapes=[pltpu.VMEM((8, depth, groups * width), jnp.bfloat16)],
        compiler_params=pltpu.CompilerParams(vmem_limit_bytes=56 * 2**20),
        cost_estimate=pl.CostEstimate(
            flops=2 * z_rows.size * groups * width,
            bytes_accessed=2 * (z_rows.size + 3 * own.size),
            transcendentals=0,
        ),
    )(z_rows, own, other)


def dot_right(flips, z_rows, own, other):
    groups, steps, depth, width = own.shape
    return pl.pallas_call(
        functools.partial(dot_kernel, flips),
        in_specs=[pl.BlockSpec(memory_space=pl.ANY)] + [pl.BlockSpec(memory_space=pltpu.VMEM)] * 2,
        out_specs=pl.BlockSpec(memory_space=pltpu.VMEM),
        out_shape=jax.ShapeDtypeStruct((groups, 2, depth, width), jnp.bfloat16),
        scratch_shapes=[
            pltpu.VMEM((8,) + z_rows.shape[1:], jnp.bfloat16),
            pltpu.SemaphoreType.DMA((8,)),
        ],
        compiler_params=pltpu.CompilerParams(vmem_limit_bytes=32 * 2**20),
        cost_estimate=pl.CostEstimate(
            flops=z_rows.size * groups * width,
            bytes_accessed=z_rows.size + 5 * own.size,
            transcendentals=0,
        ),
    )(z_rows, own, other)


def other_core(block):
    return lax.ppermute(block, "c", SWAP)


def make_shift(product, order, first_col):
    at = lax.axis_index
    rows = product.shape[1]
    row_ids = (
        lax.broadcasted_iota(jnp.int32, product.shape, 0) * 2048
        + at("y") // 2 * 1024
        + at("c") * 512
        + at("y") % 2 * rows
        + lax.broadcasted_iota(jnp.int32, product.shape, 1)
    )
    col_ids = first_col + lax.broadcasted_iota(jnp.int32, product.shape, 2)
    ident = jnp.where(row_ids == col_ids, 1.5, 0.0).astype(jnp.float32)
    poly = lax.reduce_precision(ident - 0.5 / order * product, 8, 7)
    return (poly - ident).astype(jnp.bfloat16)


def shards(z_iter, y_iter):
    at = lax.axis_index
    order = z_iter.shape[1] * lax.axis_size("x") * lax.axis_size("zl")
    z_half = z_iter.astype(jnp.bfloat16)
    y_half = y_iter.astype(jnp.bfloat16)
    z_rows = lax.all_gather(z_half, AXES, axis_index_groups=Z_RINGS)

    zh = at("zh")
    low = zh == 0
    first_col = at("x") * 2048 + at("zl") * 256 + zh * 128
    left, right = y_half[:, :128], y_half[:, 128:]
    mine = jnp.where(low, left, right)
    yours = lax.ppermute(jnp.where(low, right, left), "zh", SWAP)
    y_both = jnp.stack([jnp.where(low, mine, yours), jnp.where(low, yours, mine)])
    y_both = y_both.reshape(4, 256, 128)

    turn = [(i * 4 + j, j * 4 + i) for i in range(4) for j in range(4)]
    turned = lax.ppermute(y_both, PLANE, turn)
    y_own = lax.all_to_all(jnp.stack([turned] * 4), "y", 0, 0, tiled=True)
    part = dot_right_all(z_rows, y_own, other_core(y_own))

    part = lax.all_to_all(part.reshape(16, 256, 128), PLANE, 0, 0, tiled=True)
    product = part.reshape(4, 4, 256, 128).astype(jnp.float32).sum(0)
    shift = make_shift(product, order, first_col)

    spread = jnp.broadcast_to(shift[:, None], (4, 4, 256, 128)).reshape(16, 256, 128)
    own = lax.all_to_all(spread, PLANE, 0, 0, tiled=True).reshape(4, 4, 256, 128)
    other = other_core(own)

    def sum_x(part):
        part = lax.all_to_all(part, "x", 0, 0, tiled=True)
        return part.astype(jnp.float32).sum(0).reshape(512, 128)

    yours = sum_x(dot_right(1, z_rows, own, other)).astype(jnp.bfloat16)
    mine = dot_right(0, z_rows, own, other)
    yours = lax.ppermute(yours, "zh", SWAP).astype(jnp.float32)
    mine = sum_x(mine)
    part = jnp.concatenate([jnp.where(low, mine, yours), jnp.where(low, yours, mine)], axis=1)
    return 1.5 * z_half.astype(jnp.float32) + part


def solution(mesh):
    fine = Mesh(mesh.devices.reshape(SIZES), AXES)
    spec = P(("y", "zh", "c"), ("x", "zl"))
    return jax.shard_map(
        shards,
        mesh=fine,
        in_specs=(spec, spec),
        out_specs=spec,
        check_vma=False,
    )
```

```python
import functools

import jax
import jax.numpy as jnp
from jax import lax
from jax.experimental import pallas as pl
from jax.experimental.pallas import tpu as pltpu
from jax.sharding import Mesh
from jax.sharding import PartitionSpec as P

AXES = ("x", "zl", "y", "zh", "c")
SIZES = (4, 8, 4, 2, 2)
PLANE = ("x", "y")
SWAP = [(0, 1), (1, 0)]


def flat_id(x, zl, y, zh, c):
    return (((x * 8 + zl) * 4 + y) * 2 + zh) * 2 + c


Z_RINGS = [
    [flat_id(x, z % 8, y, z // 8, c) for z in range(16)]
    for x in range(4)
    for y in range(4)
    for c in range(2)
]


def dot_kernel(flips, z_ref, own_ref, other_ref, out_ref, left, sem):
    groups, _, depth, width = own_ref.shape
    c = lax.axis_index("c")
    first = (lax.axis_index("zh") ^ flips) * 8
    copies = []
    for n in range(8):
        chunk = (n % 4) // 2 * 4 + (c ^ (n // 4)) * 2 + n % 2
        copies.append(pltpu.make_async_copy(z_ref.at[first + chunk], left.at[n], sem.at[n]))
    for copy in copies:
        copy.start()
    for s in range(2):
        total = None
        for n in range(8):
            if s == 0:
                copies[n].wait()
            part = (own_ref, other_ref)[n // 4]
            right = jnp.concatenate([part[j, n % 4] for j in range(groups)], axis=1)
            rows = left[n, s * depth : (s + 1) * depth, :]
            term = jnp.dot(rows, right, preferred_element_type=jnp.float32)
            total = term if total is None else total + term
        for j in range(groups):
            out_ref[j, s] = total[:, j * width : (j + 1) * width].astype(out_ref.dtype)


def dot_all_kernel(z_ref, right_ref, out_ref, left, sem):
    groups, _, depth, width = out_ref.shape
    copies = [pltpu.make_async_copy(z_ref.at[n], left.at[n], sem.at[n]) for n in range(16)]
    for copy in copies:
        copy.start()
    for zh in range(2):
        for h in range(2):
            cols = slice(h * 2 * width, (h + 1) * 2 * width)
            total = None
            for k in range(8):
                if h == 0:
                    copies[zh * 8 + k].wait()
                term = jnp.dot(
                    left[zh * 8 + k], right_ref[k, :, cols], preferred_element_type=jnp.float32
                )
                total = term if total is None else total + term
            total = total.astype(out_ref.dtype)
            for s in range(2):
                for j in range(2):
                    block = total[s * depth : (s + 1) * depth, j * width : (j + 1) * width]
                    out_ref[h * 2 + j, zh * 2 + s] = block


def dot_right_all(z_rows, own, other):
    groups, steps, depth, width = own.shape
    first = lax.axis_index("c") == 0
    right = jnp.stack([jnp.where(first, own, other), jnp.where(first, other, own)])
    right = right.reshape(2, groups, 2, 2, depth, width).transpose(2, 0, 3, 4, 1, 5)
    right = right.reshape(8, depth, groups * width)
    return pl.pallas_call(
        dot_all_kernel,
        in_specs=[pl.BlockSpec(memory_space=pl.ANY), pl.BlockSpec(memory_space=pltpu.VMEM)],
        out_specs=pl.BlockSpec(memory_space=pltpu.VMEM),
        out_shape=jax.ShapeDtypeStruct(own.shape, jnp.bfloat16),
        scratch_shapes=[
            pltpu.VMEM(z_rows.shape, jnp.bfloat16),
            pltpu.SemaphoreType.DMA((16,)),
        ],
        compiler_params=pltpu.CompilerParams(vmem_limit_bytes=48 * 2**20),
        cost_estimate=pl.CostEstimate(
            flops=2 * z_rows.size * groups * width,
            bytes_accessed=2 * (z_rows.size + 3 * own.size),
            transcendentals=0,
        ),
    )(z_rows, right)


def dot_right(flips, z_rows, own, other):
    groups, steps, depth, width = own.shape
    return pl.pallas_call(
        functools.partial(dot_kernel, flips),
        in_specs=[pl.BlockSpec(memory_space=pl.ANY)] + [pl.BlockSpec(memory_space=pltpu.VMEM)] * 2,
        out_specs=pl.BlockSpec(memory_space=pltpu.VMEM),
        out_shape=jax.ShapeDtypeStruct((groups, 2, depth, width), jnp.bfloat16),
        scratch_shapes=[
            pltpu.VMEM((8,) + z_rows.shape[1:], jnp.bfloat16),
            pltpu.SemaphoreType.DMA((8,)),
        ],
        compiler_params=pltpu.CompilerParams(vmem_limit_bytes=32 * 2**20),
        cost_estimate=pl.CostEstimate(
            flops=z_rows.size * groups * width,
            bytes_accessed=z_rows.size + 5 * own.size,
            transcendentals=0,
        ),
    )(z_rows, own, other)


def other_core(block):
    return lax.ppermute(block, "c", SWAP)


def make_ident(shape, first_col):
    at = lax.axis_index
    rows = shape[1]
    row_ids = (
        lax.broadcasted_iota(jnp.int32, shape, 0) * 2048
        + at("y") // 2 * 1024
        + at("c") * 512
        + at("y") % 2 * rows
        + lax.broadcasted_iota(jnp.int32, shape, 1)
    )
    col_ids = first_col + lax.broadcasted_iota(jnp.int32, shape, 2)
    return jnp.where(row_ids == col_ids, 1.5, 0.0).astype(jnp.float32)


def make_shift(product, order, ident):
    poly = lax.reduce_precision(ident - 0.5 / order * product, 8, 7)
    return (poly - ident).astype(jnp.bfloat16)


def shards(z_iter, y_iter):
    at = lax.axis_index
    order = z_iter.shape[1] * lax.axis_size("x") * lax.axis_size("zl")
    z_half = z_iter.astype(jnp.bfloat16)
    y_half = y_iter.astype(jnp.bfloat16)
    z_rows = lax.all_gather(z_half, AXES, axis_index_groups=Z_RINGS)

    zh = at("zh")
    low = zh == 0
    first_col = at("x") * 2048 + at("zl") * 256 + zh * 128
    left, right = y_half[:, :128], y_half[:, 128:]
    mine = jnp.where(low, left, right)
    yours = lax.ppermute(jnp.where(low, right, left), "zh", SWAP)
    y_both = jnp.stack([jnp.where(low, mine, yours), jnp.where(low, yours, mine)])
    y_both = y_both.reshape(4, 256, 128)

    turn = [(i * 4 + j, j * 4 + i) for i in range(4) for j in range(4)]
    turned = lax.ppermute(y_both, PLANE, turn)
    y_own = lax.all_to_all(jnp.stack([turned] * 4), "y", 0, 0, tiled=True)
    y_other = other_core(y_own)
    y_other, ident = lax.optimization_barrier((y_other, make_ident((4, 256, 128), first_col)))
    part = dot_right_all(z_rows, y_own, y_other)

    part = lax.all_to_all(part.reshape(16, 256, 128), PLANE, 0, 0, tiled=True)
    product = part.reshape(4, 4, 256, 128).astype(jnp.float32).sum(0)
    shift = make_shift(product, order, ident)

    spread = jnp.broadcast_to(shift[:, None], (4, 4, 256, 128)).reshape(16, 256, 128)
    own = lax.all_to_all(spread, PLANE, 0, 0, tiled=True).reshape(4, 4, 256, 128)
    other = other_core(own)

    def sum_x(part):
        part = lax.all_to_all(part, "x", 0, 0, tiled=True)
        return part.astype(jnp.float32).sum(0).reshape(512, 128)

    yours = sum_x(dot_right(1, z_rows, own, other)).astype(jnp.bfloat16)
    mine = dot_right(0, z_rows, own, other)
    yours = lax.ppermute(yours, "zh", SWAP).astype(jnp.float32)
    mine = sum_x(mine)
    part = jnp.concatenate([jnp.where(low, mine, yours), jnp.where(low, yours, mine)], axis=1)
    return 1.5 * z_half.astype(jnp.float32) + part


def solution(mesh):
    fine = Mesh(mesh.devices.reshape(SIZES), AXES)
    spec = P(("y", "zh", "c"), ("x", "zl"))
    return jax.shard_map(
        shards,
        mesh=fine,
        in_specs=(spec, spec),
        out_specs=spec,
        check_vma=False,
    )
```

```python
import functools

import jax
import jax.numpy as jnp
from jax import lax
from jax.experimental import pallas as pl
from jax.experimental.pallas import tpu as pltpu
from jax.sharding import Mesh
from jax.sharding import PartitionSpec as P

AXES = ("x", "zl", "y", "zh", "c")
SIZES = (4, 8, 4, 2, 2)
PLANE = ("x", "y")
SWAP = [(0, 1), (1, 0)]


def flat_id(x, zl, y, zh, c):
    return (((x * 8 + zl) * 4 + y) * 2 + zh) * 2 + c


Z_RINGS = [
    [flat_id(x, z % 8, y, z // 8, c) for z in range(16)]
    for x in range(4)
    for y in range(4)
    for c in range(2)
]


def dot_kernel(flips, z_ref, own_ref, other_ref, out_ref, left, sem):
    groups, _, depth, width = own_ref.shape
    c = lax.axis_index("c")
    first = (lax.axis_index("zh") ^ flips) * 8
    copies = []
    for n in range(8):
        chunk = (n % 4) // 2 * 4 + (c ^ (n // 4)) * 2 + n % 2
        copies.append(pltpu.make_async_copy(z_ref.at[first + chunk], left.at[n], sem.at[n]))
    for copy in copies:
        copy.start()
    for s in range(2):
        total = None
        for n in range(8):
            if s == 0:
                copies[n].wait()
            part = (own_ref, other_ref)[n // 4]
            right = jnp.concatenate([part[j, n % 4] for j in range(groups)], axis=1)
            rows = left[n, s * depth : (s + 1) * depth, :]
            term = jnp.dot(rows, right, preferred_element_type=jnp.float32)
            total = term if total is None else total + term
        for j in range(groups):
            out_ref[j, s] = total[:, j * width : (j + 1) * width].astype(out_ref.dtype)


def dot_all_kernel(z_ref, right_ref, out_ref, left, sem):
    groups, _, depth, width = out_ref.shape
    copies = [pltpu.make_async_copy(z_ref.at[n], left.at[n], sem.at[n]) for n in range(16)]
    for copy in copies:
        copy.start()
    for zh in range(2):
        for h in range(2):
            cols = slice(h * 2 * width, (h + 1) * 2 * width)
            total = None
            for k in range(8):
                if h == 0:
                    copies[zh * 8 + k].wait()
                term = jnp.dot(
                    left[zh * 8 + k], right_ref[k, :, cols], preferred_element_type=jnp.float32
                )
                total = term if total is None else total + term
            total = total.astype(out_ref.dtype)
            for s in range(2):
                for j in range(2):
                    block = total[s * depth : (s + 1) * depth, j * width : (j + 1) * width]
                    out_ref[h * 2 + j, zh * 2 + s] = block


def dot_right_all(z_rows, own, other):
    groups, steps, depth, width = own.shape
    first = lax.axis_index("c") == 0
    right = jnp.stack([jnp.where(first, own, other), jnp.where(first, other, own)])
    right = right.reshape(2, groups, 2, 2, depth, width).transpose(2, 0, 3, 4, 1, 5)
    right = right.reshape(8, depth, groups * width)
    return pl.pallas_call(
        dot_all_kernel,
        in_specs=[pl.BlockSpec(memory_space=pl.ANY), pl.BlockSpec(memory_space=pltpu.VMEM)],
        out_specs=pl.BlockSpec(memory_space=pltpu.VMEM),
        out_shape=jax.ShapeDtypeStruct(own.shape, jnp.bfloat16),
        scratch_shapes=[
            pltpu.VMEM(z_rows.shape, jnp.bfloat16),
            pltpu.SemaphoreType.DMA((16,)),
        ],
        compiler_params=pltpu.CompilerParams(vmem_limit_bytes=48 * 2**20),
        cost_estimate=pl.CostEstimate(
            flops=2 * z_rows.size * groups * width,
            bytes_accessed=2 * (z_rows.size + 3 * own.size),
            transcendentals=0,
        ),
    )(z_rows, right)


def dot_right(flips, z_rows, own, other):
    groups, steps, depth, width = own.shape
    return pl.pallas_call(
        functools.partial(dot_kernel, flips),
        in_specs=[pl.BlockSpec(memory_space=pl.ANY)] + [pl.BlockSpec(memory_space=pltpu.VMEM)] * 2,
        out_specs=pl.BlockSpec(memory_space=pltpu.VMEM),
        out_shape=jax.ShapeDtypeStruct((groups, 2, depth, width), jnp.bfloat16),
        scratch_shapes=[
            pltpu.VMEM((8,) + z_rows.shape[1:], jnp.bfloat16),
            pltpu.SemaphoreType.DMA((8,)),
        ],
        compiler_params=pltpu.CompilerParams(vmem_limit_bytes=32 * 2**20),
        cost_estimate=pl.CostEstimate(
            flops=z_rows.size * groups * width,
            bytes_accessed=z_rows.size + 5 * own.size,
            transcendentals=0,
        ),
    )(z_rows, own, other)


def other_core(block):
    return lax.ppermute(block, "c", SWAP)


def make_ident(shape, first_col):
    at = lax.axis_index
    rows = shape[1]
    row_ids = (
        lax.broadcasted_iota(jnp.int32, shape, 0) * 2048
        + at("y") // 2 * 1024
        + at("c") * 512
        + at("y") % 2 * rows
        + lax.broadcasted_iota(jnp.int32, shape, 1)
    )
    col_ids = first_col + lax.broadcasted_iota(jnp.int32, shape, 2)
    return jnp.where(row_ids == col_ids, 1.5, 0.0).astype(jnp.float32)


def make_shift(product, order, ident):
    poly = lax.reduce_precision(ident - 0.5 / order * product, 8, 7)
    return (poly - ident).astype(jnp.bfloat16)


def shards(z_iter, y_iter):
    at = lax.axis_index
    order = z_iter.shape[1] * lax.axis_size("x") * lax.axis_size("zl")
    z_half = z_iter.astype(jnp.bfloat16)
    y_half = y_iter.astype(jnp.bfloat16)
    z_rows = lax.all_gather(z_half, AXES, axis_index_groups=Z_RINGS)

    zh = at("zh")
    low = zh == 0
    first_col = at("x") * 2048 + at("zl") * 256 + zh * 128
    left, right = y_half[:, :128], y_half[:, 128:]
    mine = jnp.where(low, left, right)
    yours = lax.ppermute(jnp.where(low, right, left), "zh", SWAP)
    y_both = jnp.stack([jnp.where(low, mine, yours), jnp.where(low, yours, mine)])
    y_both = y_both.reshape(4, 256, 128)

    turn = [(i * 4 + j, j * 4 + i) for i in range(4) for j in range(4)]
    turned = lax.ppermute(y_both, PLANE, turn)
    y_own = lax.all_to_all(jnp.stack([turned] * 4), "y", 0, 0, tiled=True)
    y_other = other_core(y_own)
    y_other, ident = lax.optimization_barrier((y_other, make_ident((4, 256, 128), first_col)))
    part = dot_right_all(z_rows, y_own, y_other)

    part = lax.all_to_all(part.reshape(16, 256, 128), PLANE, 0, 0, tiled=True)
    product = part.reshape(4, 4, 256, 128).astype(jnp.float32).sum(0)
    shift = make_shift(product, order, ident)

    spread = jnp.broadcast_to(shift[:, None], (4, 4, 256, 128)).reshape(16, 256, 128)
    own = lax.all_to_all(spread, PLANE, 0, 0, tiled=True).reshape(4, 4, 256, 128)
    other = other_core(own)

    def sum_x(part):
        part = lax.all_to_all(part, "x", 0, 0, tiled=True)
        return part.astype(jnp.float32).sum(0).reshape(512, 128)

    yours = sum_x(dot_right(1, z_rows, own, other)).astype(jnp.bfloat16)
    mine = dot_right(0, z_rows, own, other)
    yours = lax.ppermute(yours, "zh", SWAP).astype(jnp.float32)
    mine = lax.cond(
        at("c") < 2, sum_x, lambda part: jnp.zeros((512, 128), jnp.float32), mine
    )
    part = jnp.concatenate([jnp.where(low, mine, yours), jnp.where(low, yours, mine)], axis=1)
    return 1.5 * lax.reduce_precision(z_iter, 8, 7) + part


def solution(mesh):
    fine = Mesh(mesh.devices.reshape(SIZES), AXES)
    spec = P(("y", "zh", "c"), ("x", "zl"))
    return jax.shard_map(
        shards,
        mesh=fine,
        in_specs=(spec, spec),
        out_specs=spec,
        check_vma=False,
    )
```

```python
import functools

import jax
import jax.numpy as jnp
from jax import lax
from jax.experimental import pallas as pl
from jax.experimental.pallas import tpu as pltpu
from jax.sharding import Mesh
from jax.sharding import PartitionSpec as P

AXES = ("x", "zl", "y", "zh", "c")
SIZES = (4, 8, 4, 2, 2)
PLANE = ("x", "y")
SWAP = [(0, 1), (1, 0)]


def flat_id(x, zl, y, zh, c):
    return (((x * 8 + zl) * 4 + y) * 2 + zh) * 2 + c


Z_RINGS = [
    [flat_id(x, z % 8, y, z // 8, c) for z in range(16)]
    for x in range(4)
    for y in range(4)
    for c in range(2)
]


def dot_kernel(flips, z_ref, own_ref, other_ref, out_ref):
    groups, _, depth, width = own_ref.shape
    c = lax.axis_index("c")
    first = (lax.axis_index("zh") ^ flips) * 8
    for s in range(2):
        total = None
        for n in range(8):
            part = (own_ref, other_ref)[n // 4]
            right = jnp.concatenate([part[j, n % 4] for j in range(groups)], axis=1)
            chunk = first + (n % 4) // 2 * 4 + (c ^ (n // 4)) * 2 + n % 2
            rows = z_ref[chunk, s * depth : (s + 1) * depth, :]
            term = jnp.dot(rows, right, preferred_element_type=jnp.float32)
            total = term if total is None else total + term
        for j in range(groups):
            out_ref[j, s] = total[:, j * width : (j + 1) * width].astype(out_ref.dtype)


def dot_all_kernel(z_ref, right_ref, out_ref, left, sem):
    groups, _, depth, width = out_ref.shape
    copies = [pltpu.make_async_copy(z_ref.at[n], left.at[n], sem.at[n]) for n in range(16)]
    ahead = 4
    for copy in copies[:ahead]:
        copy.start()
    for zh in range(2):
        for h in range(2):
            cols = slice(h * 2 * width, (h + 1) * 2 * width)
            total = None
            for k in range(8):
                if h == 0:
                    copies[zh * 8 + k].wait()
                    if zh * 8 + k + ahead < 16:
                        copies[zh * 8 + k + ahead].start()
                term = jnp.dot(
                    left[zh * 8 + k], right_ref[k, :, cols], preferred_element_type=jnp.float32
                )
                total = term if total is None else total + term
            total = total.astype(out_ref.dtype)
            for s in range(2):
                for j in range(2):
                    block = total[s * depth : (s + 1) * depth, j * width : (j + 1) * width]
                    out_ref[h * 2 + j, zh * 2 + s] = block


def dot_right_all(z_rows, own, other):
    groups, steps, depth, width = own.shape
    first = lax.axis_index("c") == 0
    right = jnp.stack([jnp.where(first, own, other), jnp.where(first, other, own)])
    right = right.reshape(2, groups, 2, 2, depth, width).transpose(2, 0, 3, 4, 1, 5)
    right = right.reshape(8, depth, groups * width)
    return pl.pallas_call(
        dot_all_kernel,
        in_specs=[pl.BlockSpec(memory_space=pl.ANY), pl.BlockSpec(memory_space=pltpu.VMEM)],
        out_specs=pl.BlockSpec(memory_space=pltpu.VMEM),
        out_shape=jax.ShapeDtypeStruct(own.shape, jnp.bfloat16),
        scratch_shapes=[
            pltpu.VMEM(z_rows.shape, jnp.bfloat16),
            pltpu.SemaphoreType.DMA((16,)),
        ],
        compiler_params=pltpu.CompilerParams(vmem_limit_bytes=48 * 2**20),
        cost_estimate=pl.CostEstimate(
            flops=2 * z_rows.size * groups * width,
            bytes_accessed=2 * (z_rows.size + 3 * own.size),
            transcendentals=0,
        ),
    )(z_rows, right)


def dot_right(flips, z_rows, own, other):
    groups, steps, depth, width = own.shape
    return pl.pallas_call(
        functools.partial(dot_kernel, flips),
        in_specs=[pl.BlockSpec(memory_space=pltpu.VMEM)] * 3,
        out_specs=pl.BlockSpec(memory_space=pltpu.VMEM),
        out_shape=jax.ShapeDtypeStruct((groups, 2, depth, width), jnp.bfloat16),
        compiler_params=pltpu.CompilerParams(vmem_limit_bytes=32 * 2**20),
        cost_estimate=pl.CostEstimate(
            flops=z_rows.size * groups * width,
            bytes_accessed=z_rows.size + 5 * own.size,
            transcendentals=0,
        ),
    )(z_rows, own, other)


def other_core(block):
    return lax.ppermute(block, "c", SWAP)


def make_ident(shape, first_col):
    at = lax.axis_index
    rows = shape[1]
    row_ids = (
        lax.broadcasted_iota(jnp.int32, shape, 0) * 2048
        + at("y") // 2 * 1024
        + at("c") * 512
        + at("y") % 2 * rows
        + lax.broadcasted_iota(jnp.int32, shape, 1)
    )
    col_ids = first_col + lax.broadcasted_iota(jnp.int32, shape, 2)
    return jnp.where(row_ids == col_ids, 1.5, 0.0).astype(jnp.float32)


def make_shift(product, order, ident):
    poly = lax.reduce_precision(ident - 0.5 / order * product, 8, 7)
    return (poly - ident).astype(jnp.bfloat16)


def shards(z_iter, y_iter):
    at = lax.axis_index
    order = z_iter.shape[1] * lax.axis_size("x") * lax.axis_size("zl")
    z_half = z_iter.astype(jnp.bfloat16)
    y_half = y_iter.astype(jnp.bfloat16)
    z_rows = lax.all_gather(z_half, AXES, axis_index_groups=Z_RINGS)

    zh = at("zh")
    low = zh == 0
    first_col = at("x") * 2048 + at("zl") * 256 + zh * 128
    left, right = y_half[:, :128], y_half[:, 128:]
    mine = jnp.where(low, left, right)
    yours = lax.ppermute(jnp.where(low, right, left), "zh", SWAP)
    y_both = jnp.stack([jnp.where(low, mine, yours), jnp.where(low, yours, mine)])
    y_both = y_both.reshape(4, 256, 128)

    turn = [(i * 4 + j, j * 4 + i) for i in range(4) for j in range(4)]
    turned = lax.ppermute(y_both, PLANE, turn)
    y_own = lax.all_to_all(jnp.stack([turned] * 4), "y", 0, 0, tiled=True)
    y_other = other_core(y_own)
    y_other, ident = lax.optimization_barrier((y_other, make_ident((4, 256, 128), first_col)))
    part = dot_right_all(z_rows, y_own, y_other)

    part = lax.all_to_all(part.reshape(16, 256, 128), PLANE, 0, 0, tiled=True)
    product = part.reshape(4, 4, 256, 128).astype(jnp.float32).sum(0)
    shift = make_shift(product, order, ident)

    spread = jnp.broadcast_to(shift[:, None], (4, 4, 256, 128)).reshape(16, 256, 128)
    own = lax.all_to_all(spread, PLANE, 0, 0, tiled=True).reshape(4, 4, 256, 128)
    other = other_core(own)

    def sum_x(part):
        part = lax.all_to_all(part, "x", 0, 0, tiled=True)
        return part.astype(jnp.float32).sum(0).reshape(512, 128)

    yours = sum_x(dot_right(1, z_rows, own, other)).astype(jnp.bfloat16)
    mine = dot_right(0, z_rows, own, other)
    yours = lax.ppermute(yours, "zh", SWAP).astype(jnp.float32)
    mine = lax.cond(
        at("c") < 2, sum_x, lambda part: jnp.zeros((512, 128), jnp.float32), mine
    )
    part = jnp.concatenate([jnp.where(low, mine, yours), jnp.where(low, yours, mine)], axis=1)
    return 1.5 * lax.reduce_precision(z_iter, 8, 7) + part


def solution(mesh):
    fine = Mesh(mesh.devices.reshape(SIZES), AXES)
    spec = P(("y", "zh", "c"), ("x", "zl"))
    return jax.shard_map(
        shards,
        mesh=fine,
        in_specs=(spec, spec),
        out_specs=spec,
        check_vma=False,
    )
```

```python
import functools

import jax
import jax.numpy as jnp
from jax import lax
from jax.experimental import pallas as pl
from jax.experimental.pallas import tpu as pltpu
from jax.sharding import Mesh
from jax.sharding import PartitionSpec as P

AXES = ("x", "zl", "y", "zh", "c")
SIZES = (4, 8, 4, 2, 2)
PLANE = ("x", "y")
SWAP = [(0, 1), (1, 0)]


def flat_id(x, zl, y, zh, c):
    return (((x * 8 + zl) * 4 + y) * 2 + zh) * 2 + c


Z_RINGS = [
    [flat_id(x, z % 8, y, z // 8, c) for z in range(16)]
    for x in range(4)
    for y in range(4)
    for c in range(2)
]


def dot_kernel(flips, z_ref, own_ref, other_ref, out_ref):
    groups, _, depth, width = own_ref.shape
    c = lax.axis_index("c")
    first = (lax.axis_index("zh") ^ flips) * 8
    for s in range(2):
        total = None
        for n in range(8):
            part = (own_ref, other_ref)[n // 4]
            right = jnp.concatenate([part[j, n % 4] for j in range(groups)], axis=1)
            chunk = first + (n % 4) // 2 * 4 + (c ^ (n // 4)) * 2 + n % 2
            rows = z_ref[chunk, s * depth : (s + 1) * depth, :]
            term = jnp.dot(rows, right, preferred_element_type=jnp.float32)
            total = term if total is None else total + term
        for j in range(groups):
            out_ref[j, s] = total[:, j * width : (j + 1) * width].astype(out_ref.dtype)


def dot_all_kernel(z_ref, right_ref, out_ref, left, sem):
    groups, _, depth, width = out_ref.shape
    copies = [pltpu.make_async_copy(z_ref.at[n], left.at[n], sem.at[n]) for n in range(16)]
    for copy in copies:
        copy.start()
    for zh in range(2):
        total = None
        for k in range(8):
            copies[zh * 8 + k].wait()
            term = jnp.dot(left[zh * 8 + k], right_ref[k], preferred_element_type=jnp.float32)
            total = term if total is None else total + term
        total = total.astype(out_ref.dtype)
        for s in range(2):
            for j in range(groups):
                block = total[s * depth : (s + 1) * depth, j * width : (j + 1) * width]
                out_ref[j, zh * 2 + s] = block


def dot_right_all(z_rows, own, other):
    groups, steps, depth, width = own.shape
    first = lax.axis_index("c") == 0
    right = jnp.stack([jnp.where(first, own, other), jnp.where(first, other, own)])
    right = right.reshape(2, groups, 2, 2, depth, width).transpose(2, 0, 3, 4, 1, 5)
    right = right.reshape(8, depth, groups * width)
    return pl.pallas_call(
        dot_all_kernel,
        in_specs=[pl.BlockSpec(memory_space=pl.ANY), pl.BlockSpec(memory_space=pltpu.VMEM)],
        out_specs=pl.BlockSpec(memory_space=pltpu.VMEM),
        out_shape=jax.ShapeDtypeStruct(own.shape, jnp.bfloat16),
        scratch_shapes=[
            pltpu.VMEM(z_rows.shape, jnp.bfloat16),
            pltpu.SemaphoreType.DMA((16,)),
        ],
        compiler_params=pltpu.CompilerParams(vmem_limit_bytes=48 * 2**20),
        cost_estimate=pl.CostEstimate(
            flops=2 * z_rows.size * groups * width,
            bytes_accessed=2 * (z_rows.size + 3 * own.size),
            transcendentals=0,
        ),
    )(z_rows, right)


def dot_right(flips, z_rows, own, other):
    groups, steps, depth, width = own.shape
    return pl.pallas_call(
        functools.partial(dot_kernel, flips),
        in_specs=[pl.BlockSpec(memory_space=pltpu.VMEM)] * 3,
        out_specs=pl.BlockSpec(memory_space=pltpu.VMEM),
        out_shape=jax.ShapeDtypeStruct((groups, 2, depth, width), jnp.bfloat16),
        compiler_params=pltpu.CompilerParams(vmem_limit_bytes=32 * 2**20),
        cost_estimate=pl.CostEstimate(
            flops=z_rows.size * groups * width,
            bytes_accessed=z_rows.size + 5 * own.size,
            transcendentals=0,
        ),
    )(z_rows, own, other)


def other_core(block):
    return lax.ppermute(block, "c", SWAP)


def make_ident(shape, first_col):
    at = lax.axis_index
    rows = shape[1]
    row_ids = (
        lax.broadcasted_iota(jnp.int32, shape, 0) * 2048
        + at("y") // 2 * 1024
        + at("c") * 512
        + at("y") % 2 * rows
        + lax.broadcasted_iota(jnp.int32, shape, 1)
    )
    col_ids = first_col + lax.broadcasted_iota(jnp.int32, shape, 2)
    return jnp.where(row_ids == col_ids, 1.5, 0.0).astype(jnp.float32)


def make_shift(product, order, ident):
    poly = lax.reduce_precision(ident - 0.5 / order * product, 8, 7)
    return (poly - ident).astype(jnp.bfloat16)


def shards(z_iter, y_iter):
    at = lax.axis_index
    order = z_iter.shape[1] * lax.axis_size("x") * lax.axis_size("zl")
    z_half = z_iter.astype(jnp.bfloat16)
    y_half = y_iter.astype(jnp.bfloat16)
    z_rows = lax.all_gather(z_half, AXES, axis_index_groups=Z_RINGS)

    zh = at("zh")
    low = zh == 0
    first_col = at("x") * 2048 + at("zl") * 256 + zh * 128
    left, right = y_half[:, :128], y_half[:, 128:]
    mine = jnp.where(low, left, right)
    yours = lax.ppermute(jnp.where(low, right, left), "zh", SWAP)
    y_both = jnp.stack([jnp.where(low, mine, yours), jnp.where(low, yours, mine)])
    y_both = y_both.reshape(4, 256, 128)

    turn = [(i * 4 + j, j * 4 + i) for i in range(4) for j in range(4)]
    turned = lax.ppermute(y_both, PLANE, turn)
    y_own = lax.all_to_all(jnp.stack([turned] * 4), "y", 0, 0, tiled=True)
    y_other = other_core(y_own)
    y_other, ident = lax.optimization_barrier((y_other, make_ident((4, 256, 128), first_col)))
    part = dot_right_all(z_rows, y_own, y_other)

    part = lax.all_to_all(part.reshape(16, 256, 128), PLANE, 0, 0, tiled=True)
    product = part.reshape(4, 4, 256, 128).astype(jnp.float32).sum(0)
    shift = make_shift(product, order, ident)

    spread = jnp.broadcast_to(shift[:, None], (4, 4, 256, 128)).reshape(16, 256, 128)
    own = lax.all_to_all(spread, PLANE, 0, 0, tiled=True).reshape(4, 4, 256, 128)
    other = other_core(own)

    def sum_x(part):
        part = lax.all_to_all(part, "x", 0, 0, tiled=True)
        return part.astype(jnp.float32).sum(0).reshape(512, 128)

    yours = sum_x(dot_right(1, z_rows, own, other)).astype(jnp.bfloat16)
    mine = dot_right(0, z_rows, own, other)
    yours = lax.ppermute(yours, "zh", SWAP).astype(jnp.float32)
    mine = lax.cond(
        at("c") < 2, sum_x, lambda part: jnp.zeros((512, 128), jnp.float32), mine
    )
    part = jnp.concatenate([jnp.where(low, mine, yours), jnp.where(low, yours, mine)], axis=1)
    return 1.5 * lax.reduce_precision(z_iter, 8, 7) + part


def solution(mesh):
    fine = Mesh(mesh.devices.reshape(SIZES), AXES)
    spec = P(("y", "zh", "c"), ("x", "zl"))
    return jax.shard_map(
        shards,
        mesh=fine,
        in_specs=(spec, spec),
        out_specs=spec,
        check_vma=False,
    )
```

```python
import functools

import jax
import jax.numpy as jnp
from jax import lax
from jax.experimental import pallas as pl
from jax.experimental.pallas import tpu as pltpu
from jax.sharding import Mesh
from jax.sharding import PartitionSpec as P

AXES = ("x", "zl", "y", "zh", "c")
SIZES = (4, 8, 4, 2, 2)
PLANE = ("x", "y")
SWAP = [(0, 1), (1, 0)]


def flat_id(x, zl, y, zh, c):
    return (((x * 8 + zl) * 4 + y) * 2 + zh) * 2 + c


Z_RINGS = [
    [flat_id(x, z % 8, y, z // 8, c) for z in range(16)]
    for x in range(4)
    for y in range(4)
    for c in range(2)
]


def dot_kernel(flips, z_ref, own_ref, other_ref, out_ref):
    groups, _, depth, width = own_ref.shape
    c = lax.axis_index("c")
    first = (lax.axis_index("zh") ^ flips) * 8
    for s in range(2):
        total = None
        for n in range(8):
            part = (own_ref, other_ref)[n // 4]
            right = jnp.concatenate([part[j, n % 4] for j in range(groups)], axis=1)
            chunk = first + (n % 4) // 2 * 4 + (c ^ (n // 4)) * 2 + n % 2
            rows = z_ref[chunk, s * depth : (s + 1) * depth, :]
            term = jnp.dot(rows, right, preferred_element_type=jnp.float32)
            total = term if total is None else total + term
        for j in range(groups):
            out_ref[j, s] = total[:, j * width : (j + 1) * width].astype(out_ref.dtype)


def dot_all_kernel(z_ref, right_ref, out_ref, left, sem):
    groups, _, depth, width = out_ref.shape
    copies = [pltpu.make_async_copy(z_ref.at[n], left.at[n], sem.at[n]) for n in range(16)]
    for copy in copies:
        copy.start()
    for zh in range(2):
        total = None
        for k in range(8):
            copies[zh * 8 + k].wait()
            term = jnp.dot(left[zh * 8 + k], right_ref[k], preferred_element_type=jnp.float32)
            total = term if total is None else total + term
        total = total.astype(out_ref.dtype)
        for s in range(2):
            for j in range(groups):
                block = total[s * depth : (s + 1) * depth, j * width : (j + 1) * width]
                out_ref[j, zh * 2 + s] = block


def dot_right_all(z_rows, own, other):
    groups, steps, depth, width = own.shape
    first = lax.axis_index("c") == 0
    right = jnp.stack([jnp.where(first, own, other), jnp.where(first, other, own)])
    right = right.reshape(2, groups, 2, 2, depth, width).transpose(2, 0, 3, 4, 1, 5)
    right = right.reshape(8, depth, groups * width)
    return pl.pallas_call(
        dot_all_kernel,
        in_specs=[pl.BlockSpec(memory_space=pl.ANY), pl.BlockSpec(memory_space=pltpu.VMEM)],
        out_specs=pl.BlockSpec(memory_space=pltpu.VMEM),
        out_shape=jax.ShapeDtypeStruct(own.shape, jnp.bfloat16),
        scratch_shapes=[
            pltpu.VMEM(z_rows.shape, jnp.bfloat16),
            pltpu.SemaphoreType.DMA((16,)),
        ],
        compiler_params=pltpu.CompilerParams(vmem_limit_bytes=48 * 2**20),
        cost_estimate=pl.CostEstimate(
            flops=2 * z_rows.size * groups * width,
            bytes_accessed=2 * (z_rows.size + 3 * own.size),
            transcendentals=0,
        ),
    )(z_rows, right)


def dot_right(flips, z_rows, own, other):
    groups, steps, depth, width = own.shape
    return pl.pallas_call(
        functools.partial(dot_kernel, flips),
        in_specs=[pl.BlockSpec(memory_space=pltpu.VMEM)] * 3,
        out_specs=pl.BlockSpec(memory_space=pltpu.VMEM),
        out_shape=jax.ShapeDtypeStruct((groups, 2, depth, width), jnp.bfloat16),
        compiler_params=pltpu.CompilerParams(vmem_limit_bytes=32 * 2**20),
        cost_estimate=pl.CostEstimate(
            flops=z_rows.size * groups * width,
            bytes_accessed=z_rows.size + 5 * own.size,
            transcendentals=0,
        ),
    )(z_rows, own, other)


def other_core(block):
    return lax.ppermute(block, "c", SWAP)


def make_ident(shape, first_col):
    at = lax.axis_index
    rows = shape[1]
    row_ids = (
        lax.broadcasted_iota(jnp.int32, shape, 0) * 2048
        + at("y") // 2 * 1024
        + at("c") * 512
        + at("y") % 2 * rows
        + lax.broadcasted_iota(jnp.int32, shape, 1)
    )
    col_ids = first_col + lax.broadcasted_iota(jnp.int32, shape, 2)
    return jnp.where(row_ids == col_ids, 1.5, 0.0).astype(jnp.float32)


def make_shift(product, order, ident):
    poly = lax.reduce_precision(ident - 0.5 / order * product, 8, 7)
    return (poly - ident).astype(jnp.bfloat16)


def shards(z_iter, y_iter):
    at = lax.axis_index
    order = z_iter.shape[1] * lax.axis_size("x") * lax.axis_size("zl")
    z_half = z_iter.astype(jnp.bfloat16)
    y_half = y_iter.astype(jnp.bfloat16)
    z_rows = lax.all_gather(z_half, AXES, axis_index_groups=Z_RINGS)

    zh = at("zh")
    low = zh == 0
    first_col = at("x") * 2048 + at("zl") * 256 + zh * 128
    left, right = y_half[:, :128], y_half[:, 128:]
    mine = jnp.where(low, left, right)
    yours = lax.ppermute(jnp.where(low, right, left), "zh", SWAP)
    y_both = jnp.stack([jnp.where(low, mine, yours), jnp.where(low, yours, mine)])
    y_both = y_both.reshape(4, 256, 128)

    turn = [(i * 4 + j, j * 4 + i) for i in range(4) for j in range(4)]
    turned = lax.ppermute(y_both, PLANE, turn)
    y_own = lax.all_to_all(jnp.stack([turned] * 4), "y", 0, 0, tiled=True)
    y_other = other_core(y_own)
    y_other, ident = lax.optimization_barrier((y_other, make_ident((4, 256, 128), first_col)))
    part = dot_right_all(z_rows, y_own, y_other)

    part = lax.all_to_all(part.reshape(16, 256, 128), PLANE, 0, 0, tiled=True)
    product = part.reshape(4, 4, 256, 128).astype(jnp.float32).sum(0)
    shift = make_shift(product, order, ident)

    spread = jnp.broadcast_to(shift[:, None], (4, 4, 256, 128)).reshape(16, 256, 128)
    own = lax.all_to_all(spread, PLANE, 0, 0, tiled=True).reshape(4, 4, 256, 128)
    other = other_core(own)

    def sum_x(part):
        part = lax.all_to_all(part, "x", 0, 0, tiled=True)
        return part.astype(jnp.float32).sum(0).reshape(512, 128)

    yours = dot_right(1, z_rows, own, other)
    mine = dot_right(0, z_rows, own, other)
    yours, mine = lax.optimization_barrier((yours, mine))
    yours = sum_x(yours).astype(jnp.bfloat16)
    yours = lax.ppermute(yours, "zh", SWAP).astype(jnp.float32)
    mine = lax.cond(
        at("c") < 2, sum_x, lambda part: jnp.zeros((512, 128), jnp.float32), mine
    )
    part = jnp.concatenate([jnp.where(low, mine, yours), jnp.where(low, yours, mine)], axis=1)
    return 1.5 * lax.reduce_precision(z_iter, 8, 7) + part


def solution(mesh):
    fine = Mesh(mesh.devices.reshape(SIZES), AXES)
    spec = P(("y", "zh", "c"), ("x", "zl"))
    return jax.shard_map(
        shards,
        mesh=fine,
        in_specs=(spec, spec),
        out_specs=spec,
        check_vma=False,
    )
```

```python
import functools

import jax
import jax.numpy as jnp
from jax import lax
from jax.experimental import pallas as pl
from jax.experimental.pallas import tpu as pltpu
from jax.sharding import Mesh
from jax.sharding import PartitionSpec as P

AXES = ("x", "zl", "y", "zh", "c")
SIZES = (4, 8, 4, 2, 2)
PLANE = ("x", "y")
SWAP = [(0, 1), (1, 0)]


def flat_id(x, zl, y, zh, c):
    return (((x * 8 + zl) * 4 + y) * 2 + zh) * 2 + c


Z_RINGS = [
    [flat_id(x, z % 8, y, z // 8, c) for z in range(16)]
    for x in range(4)
    for y in range(4)
    for c in range(2)
]


def dot_kernel(flips, z_ref, own_ref, other_ref, out_ref):
    groups, _, depth, width = own_ref.shape
    c = lax.axis_index("c")
    first = (lax.axis_index("zh") ^ flips) * 8
    for s in range(2):
        total = None
        for n in range(8):
            part = (own_ref, other_ref)[n // 4]
            right = jnp.concatenate([part[j, n % 4] for j in range(groups)], axis=1)
            chunk = first + (n % 4) // 2 * 4 + (c ^ (n // 4)) * 2 + n % 2
            rows = z_ref[chunk, s * depth : (s + 1) * depth, :]
            term = jnp.dot(rows, right, preferred_element_type=jnp.float32)
            total = term if total is None else total + term
        for j in range(groups):
            out_ref[j, s] = total[:, j * width : (j + 1) * width].astype(out_ref.dtype)


def dot_all_kernel(z_ref, right_ref, out_ref, left, sem):
    groups, _, depth, width = out_ref.shape
    copies = [pltpu.make_async_copy(z_ref.at[n], left.at[n], sem.at[n]) for n in range(16)]
    for copy in copies:
        copy.start()
    for zh in range(2):
        total = None
        for k in range(8):
            copies[zh * 8 + k].wait()
            term = jnp.dot(left[zh * 8 + k], right_ref[k], preferred_element_type=jnp.float32)
            total = term if total is None else total + term
        total = total.astype(out_ref.dtype)
        for s in range(2):
            for j in range(groups):
                block = total[s * depth : (s + 1) * depth, j * width : (j + 1) * width]
                out_ref[j, zh * 2 + s] = block


def dot_right_all(z_rows, own, other):
    groups, steps, depth, width = own.shape
    first = lax.axis_index("c") == 0
    right = jnp.stack([jnp.where(first, own, other), jnp.where(first, other, own)])
    right = right.reshape(2, groups, 2, 2, depth, width).transpose(2, 0, 3, 4, 1, 5)
    right = right.reshape(8, depth, groups * width)
    return pl.pallas_call(
        dot_all_kernel,
        in_specs=[pl.BlockSpec(memory_space=pl.ANY), pl.BlockSpec(memory_space=pltpu.VMEM)],
        out_specs=pl.BlockSpec(memory_space=pltpu.VMEM),
        out_shape=jax.ShapeDtypeStruct(own.shape, jnp.bfloat16),
        scratch_shapes=[
            pltpu.VMEM(z_rows.shape, jnp.bfloat16),
            pltpu.SemaphoreType.DMA((16,)),
        ],
        compiler_params=pltpu.CompilerParams(vmem_limit_bytes=48 * 2**20),
        cost_estimate=pl.CostEstimate(
            flops=2 * z_rows.size * groups * width,
            bytes_accessed=2 * (z_rows.size + 3 * own.size),
            transcendentals=0,
        ),
    )(z_rows, right)


def dot_right(flips, z_rows, own, other):
    groups, steps, depth, width = own.shape
    return pl.pallas_call(
        functools.partial(dot_kernel, flips),
        in_specs=[pl.BlockSpec(memory_space=pltpu.VMEM)] * 3,
        out_specs=pl.BlockSpec(memory_space=pltpu.VMEM),
        out_shape=jax.ShapeDtypeStruct((groups, 2, depth, width), jnp.bfloat16),
        compiler_params=pltpu.CompilerParams(vmem_limit_bytes=32 * 2**20),
        cost_estimate=pl.CostEstimate(
            flops=z_rows.size * groups * width,
            bytes_accessed=z_rows.size + 5 * own.size,
            transcendentals=0,
        ),
    )(z_rows, own, other)


def other_core(block):
    return lax.ppermute(block, "c", SWAP)


def make_ident(shape, first_col):
    at = lax.axis_index
    rows = shape[1]
    row_ids = (
        lax.broadcasted_iota(jnp.int32, shape, 0) * 2048
        + at("y") // 2 * 1024
        + at("c") * 512
        + at("y") % 2 * rows
        + lax.broadcasted_iota(jnp.int32, shape, 1)
    )
    col_ids = first_col + lax.broadcasted_iota(jnp.int32, shape, 2)
    return jnp.where(row_ids == col_ids, 1.5, 0.0).astype(jnp.float32)


def make_shift(product, order, ident):
    poly = lax.reduce_precision(ident - 0.5 / order * product, 8, 7)
    return (poly - ident).astype(jnp.bfloat16)


def shards(z_iter, y_iter):
    at = lax.axis_index
    order = z_iter.shape[1] * lax.axis_size("x") * lax.axis_size("zl")
    z_half = z_iter.astype(jnp.bfloat16)
    y_half = y_iter.astype(jnp.bfloat16)
    z_rows = lax.all_gather(z_half, AXES, axis_index_groups=Z_RINGS)

    zh = at("zh")
    low = zh == 0
    first_col = at("x") * 2048 + at("zl") * 256 + zh * 128
    left, right = y_half[:, :128], y_half[:, 128:]
    turn = [(i * 4 + j, j * 4 + i) for i in range(4) for j in range(4)]
    turn_swap = [(a * 2 + h, b * 2 + 1 - h) for a, b in turn for h in range(2)]
    yours = lax.ppermute(jnp.where(low, right, left), PLANE + ("zh",), turn_swap)
    mine = lax.ppermute(jnp.where(low, left, right), PLANE, turn)
    y_both = jnp.stack([jnp.where(low, mine, yours), jnp.where(low, yours, mine)])
    y_both = y_both.reshape(4, 256, 128)
    y_own = lax.all_to_all(jnp.stack([y_both] * 4), "y", 0, 0, tiled=True)
    y_other = other_core(y_own)
    y_other, ident = lax.optimization_barrier((y_other, make_ident((4, 256, 128), first_col)))
    part = dot_right_all(z_rows, y_own, y_other)

    part = lax.all_to_all(part.reshape(16, 256, 128), PLANE, 0, 0, tiled=True)
    product = part.reshape(4, 4, 256, 128).astype(jnp.float32).sum(0)
    shift = make_shift(product, order, ident)

    spread = jnp.broadcast_to(shift[:, None], (4, 4, 256, 128)).reshape(16, 256, 128)
    own = lax.all_to_all(spread, PLANE, 0, 0, tiled=True).reshape(4, 4, 256, 128)
    other = other_core(own)

    def sum_x(part):
        part = lax.all_to_all(part, "x", 0, 0, tiled=True)
        return part.astype(jnp.float32).sum(0).reshape(512, 128)

    yours = sum_x(dot_right(1, z_rows, own, other)).astype(jnp.bfloat16)
    mine = dot_right(0, z_rows, own, other)
    yours = lax.ppermute(yours, "zh", SWAP).astype(jnp.float32)
    mine = lax.cond(
        at("c") < 2, sum_x, lambda part: jnp.zeros((512, 128), jnp.float32), mine
    )
    part = jnp.concatenate([jnp.where(low, mine, yours), jnp.where(low, yours, mine)], axis=1)
    return 1.5 * lax.reduce_precision(z_iter, 8, 7) + part


def solution(mesh):
    fine = Mesh(mesh.devices.reshape(SIZES), AXES)
    spec = P(("y", "zh", "c"), ("x", "zl"))
    return jax.shard_map(
        shards,
        mesh=fine,
        in_specs=(spec, spec),
        out_specs=spec,
        check_vma=False,
    )
```

```python
import functools

import jax
import jax.numpy as jnp
from jax import lax
from jax.experimental import pallas as pl
from jax.experimental.pallas import tpu as pltpu
from jax.sharding import Mesh
from jax.sharding import PartitionSpec as P

AXES = ("x", "zl", "y", "zh", "c")
SIZES = (4, 8, 4, 2, 2)
PLANE = ("x", "y")
SWAP = [(0, 1), (1, 0)]


def flat_id(x, zl, y, zh, c):
    return (((x * 8 + zl) * 4 + y) * 2 + zh) * 2 + c


Z_RINGS = [
    [flat_id(x, z % 8, y, z // 8, c) for z in range(16)]
    for x in range(4)
    for y in range(4)
    for c in range(2)
]


def dot_kernel(flips, z_ref, own_ref, other_ref, out_ref):
    groups, _, depth, width = own_ref.shape
    c = lax.axis_index("c")
    first = (lax.axis_index("zh") ^ flips) * 8
    for s in range(2):
        total = None
        for n in range(8):
            part = (own_ref, other_ref)[n // 4]
            right = jnp.concatenate([part[j, n % 4] for j in range(groups)], axis=1)
            chunk = first + (n % 4) // 2 * 4 + (c ^ (n // 4)) * 2 + n % 2
            rows = z_ref[chunk, s * depth : (s + 1) * depth, :]
            term = jnp.dot(rows, right, preferred_element_type=jnp.float32)
            total = term if total is None else total + term
        for j in range(groups):
            out_ref[j, s] = total[:, j * width : (j + 1) * width].astype(out_ref.dtype)


def dot_all_kernel(z_ref, right_ref, out_ref, left, sem):
    groups, _, depth, width = out_ref.shape
    copies = [pltpu.make_async_copy(z_ref.at[n], left.at[n], sem.at[n]) for n in range(16)]
    for copy in copies:
        copy.start()
    for zh in range(2):
        total = None
        for k in range(8):
            copies[zh * 8 + k].wait()
            term = jnp.dot(left[zh * 8 + k], right_ref[k], preferred_element_type=jnp.float32)
            total = term if total is None else total + term
        total = total.astype(out_ref.dtype)
        for s in range(2):
            for j in range(groups):
                block = total[s * depth : (s + 1) * depth, j * width : (j + 1) * width]
                out_ref[j, zh * 2 + s] = block


def dot_right_all(z_rows, own, other):
    groups, steps, depth, width = own.shape
    first = lax.axis_index("c") == 0
    right = jnp.stack([jnp.where(first, own, other), jnp.where(first, other, own)])
    right = right.reshape(2, groups, 2, 2, depth, width).transpose(2, 0, 3, 4, 1, 5)
    right = right.reshape(8, depth, groups * width)
    return pl.pallas_call(
        dot_all_kernel,
        in_specs=[pl.BlockSpec(memory_space=pl.ANY), pl.BlockSpec(memory_space=pltpu.VMEM)],
        out_specs=pl.BlockSpec(memory_space=pltpu.VMEM),
        out_shape=jax.ShapeDtypeStruct(own.shape, jnp.bfloat16),
        scratch_shapes=[
            pltpu.VMEM(z_rows.shape, jnp.bfloat16),
            pltpu.SemaphoreType.DMA((16,)),
        ],
        compiler_params=pltpu.CompilerParams(vmem_limit_bytes=48 * 2**20),
        cost_estimate=pl.CostEstimate(
            flops=2 * z_rows.size * groups * width,
            bytes_accessed=2 * (z_rows.size + 3 * own.size),
            transcendentals=0,
        ),
    )(z_rows, right)


def dot_right(flips, z_rows, own, other):
    groups, steps, depth, width = own.shape
    return pl.pallas_call(
        functools.partial(dot_kernel, flips),
        in_specs=[pl.BlockSpec(memory_space=pltpu.VMEM)] * 3,
        out_specs=pl.BlockSpec(memory_space=pltpu.VMEM),
        out_shape=jax.ShapeDtypeStruct((groups, 2, depth, width), jnp.bfloat16),
        compiler_params=pltpu.CompilerParams(vmem_limit_bytes=32 * 2**20),
        cost_estimate=pl.CostEstimate(
            flops=z_rows.size * groups * width,
            bytes_accessed=z_rows.size + 5 * own.size,
            transcendentals=0,
        ),
    )(z_rows, own, other)


def other_core(block):
    return lax.ppermute(block, "c", SWAP)


def make_ident(shape, first_col):
    at = lax.axis_index
    rows = shape[1]
    row_ids = (
        lax.broadcasted_iota(jnp.int32, shape, 0) * 2048
        + at("y") // 2 * 1024
        + at("c") * 512
        + at("y") % 2 * rows
        + lax.broadcasted_iota(jnp.int32, shape, 1)
    )
    col_ids = first_col + lax.broadcasted_iota(jnp.int32, shape, 2)
    return jnp.where(row_ids == col_ids, 1.5, 0.0).astype(jnp.float32)


def make_shift(product, order, ident):
    poly = lax.reduce_precision(ident - 0.5 / order * product, 8, 7)
    return (poly - ident).astype(jnp.bfloat16)


def shards(z_iter, y_iter):
    at = lax.axis_index
    order = z_iter.shape[1] * lax.axis_size("x") * lax.axis_size("zl")
    z_half = z_iter.astype(jnp.bfloat16)
    y_half = y_iter.astype(jnp.bfloat16)
    z_rows = lax.all_gather(z_half, AXES, axis_index_groups=Z_RINGS)

    zh = at("zh")
    low = zh == 0
    first_col = at("x") * 2048 + at("zl") * 256 + zh * 128
    left, right = y_half[:, :128], y_half[:, 128:]
    mine = jnp.where(low, left, right)
    yours = lax.ppermute(jnp.where(low, right, left), "zh", SWAP)
    y_both = jnp.stack([jnp.where(low, mine, yours), jnp.where(low, yours, mine)])
    y_both = y_both.reshape(4, 256, 128)

    turn = [(i * 4 + j, j * 4 + i) for i in range(4) for j in range(4)]
    turned = lax.ppermute(y_both, PLANE, turn)
    y_own = lax.all_to_all(jnp.stack([turned] * 4), "y", 0, 0, tiled=True)
    y_other = other_core(y_own)
    y_other, ident = lax.optimization_barrier((y_other, make_ident((4, 256, 128), first_col)))
    part = dot_right_all(z_rows, y_own, y_other)

    def branch(step, block):
        shape = jax.eval_shape(step, block)
        return lax.cond(at("c") < 2, step, lambda b: jnp.zeros(shape.shape, shape.dtype), block)

    def exchange(block):
        return lax.all_to_all(block, PLANE, 0, 0, tiled=True)

    part = branch(exchange, part.reshape(16, 256, 128))
    product = part.reshape(4, 4, 256, 128).astype(jnp.float32).sum(0)
    shift = make_shift(product, order, ident)

    spread = jnp.broadcast_to(shift[:, None], (4, 4, 256, 128)).reshape(16, 256, 128)
    own = branch(exchange, spread).reshape(4, 4, 256, 128)
    other = other_core(own)

    def sum_x(part):
        part = lax.all_to_all(part, "x", 0, 0, tiled=True)
        return part.astype(jnp.float32).sum(0).reshape(512, 128)

    yours = branch(sum_x, dot_right(1, z_rows, own, other)).astype(jnp.bfloat16)
    mine = dot_right(0, z_rows, own, other)
    yours = lax.ppermute(yours, "zh", SWAP).astype(jnp.float32)
    mine = branch(sum_x, mine)
    part = jnp.concatenate([jnp.where(low, mine, yours), jnp.where(low, yours, mine)], axis=1)
    return 1.5 * lax.reduce_precision(z_iter, 8, 7) + part


def solution(mesh):
    fine = Mesh(mesh.devices.reshape(SIZES), AXES)
    spec = P(("y", "zh", "c"), ("x", "zl"))
    return jax.shard_map(
        shards,
        mesh=fine,
        in_specs=(spec, spec),
        out_specs=spec,
        check_vma=False,
    )
```

```python
import functools

import jax
import jax.numpy as jnp
from jax import lax
from jax.experimental import pallas as pl
from jax.experimental.pallas import tpu as pltpu
from jax.sharding import Mesh
from jax.sharding import PartitionSpec as P

AXES = ("x", "zl", "y", "zh", "c")
SIZES = (4, 8, 4, 2, 2)
PLANE = ("x", "y")
SWAP = [(0, 1), (1, 0)]


def flat_id(x, zl, y, zh, c):
    return (((x * 8 + zl) * 4 + y) * 2 + zh) * 2 + c


Z_RINGS = [
    [flat_id(x, z % 8, y, z // 8, c) for z in range(16)]
    for x in range(4)
    for y in range(4)
    for c in range(2)
]


def dot_kernel(flips, z_ref, own_ref, other_ref, out_ref):
    groups, _, depth, width = own_ref.shape
    c = lax.axis_index("c")
    first = (lax.axis_index("zh") ^ flips) * 8
    for s in range(2):
        total = None
        for n in range(8):
            part = (own_ref, other_ref)[n // 4]
            right = jnp.concatenate([part[j, n % 4] for j in range(groups)], axis=1)
            chunk = first + (n % 4) // 2 * 4 + (c ^ (n // 4)) * 2 + n % 2
            rows = z_ref[chunk, s * depth : (s + 1) * depth, :]
            term = jnp.dot(rows, right, preferred_element_type=jnp.float32)
            total = term if total is None else total + term
        for j in range(groups):
            out_ref[j, s] = total[:, j * width : (j + 1) * width].astype(out_ref.dtype)


def dot_all_kernel(z_ref, right_ref, out_ref, left, sem):
    groups, _, depth, width = out_ref.shape
    copies = [pltpu.make_async_copy(z_ref.at[n], left.at[n], sem.at[n]) for n in range(16)]
    for copy in copies:
        copy.start()
    for zh in range(2):
        total = None
        for k in range(8):
            copies[zh * 8 + k].wait()
            term = jnp.dot(left[zh * 8 + k], right_ref[k], preferred_element_type=jnp.float32)
            total = term if total is None else total + term
        total = total.astype(out_ref.dtype)
        for s in range(2):
            for j in range(groups):
                block = total[s * depth : (s + 1) * depth, j * width : (j + 1) * width]
                out_ref[j, zh * 2 + s] = block


def dot_right_all(z_rows, own, other):
    groups, steps, depth, width = own.shape
    first = lax.axis_index("c") == 0
    right = jnp.stack([jnp.where(first, own, other), jnp.where(first, other, own)])
    right = right.reshape(2, groups, 2, 2, depth, width).transpose(2, 0, 3, 4, 1, 5)
    right = right.reshape(8, depth, groups * width)
    return pl.pallas_call(
        dot_all_kernel,
        in_specs=[pl.BlockSpec(memory_space=pl.ANY), pl.BlockSpec(memory_space=pltpu.VMEM)],
        out_specs=pl.BlockSpec(memory_space=pltpu.VMEM),
        out_shape=jax.ShapeDtypeStruct(own.shape, jnp.bfloat16),
        scratch_shapes=[
            pltpu.VMEM(z_rows.shape, jnp.bfloat16),
            pltpu.SemaphoreType.DMA((16,)),
        ],
        compiler_params=pltpu.CompilerParams(vmem_limit_bytes=48 * 2**20),
        cost_estimate=pl.CostEstimate(
            flops=2 * z_rows.size * groups * width,
            bytes_accessed=2 * (z_rows.size + 3 * own.size),
            transcendentals=0,
        ),
    )(z_rows, right)


def dot_right(flips, z_rows, own, other):
    groups, steps, depth, width = own.shape
    return pl.pallas_call(
        functools.partial(dot_kernel, flips),
        in_specs=[pl.BlockSpec(memory_space=pltpu.VMEM)] * 3,
        out_specs=pl.BlockSpec(memory_space=pltpu.VMEM),
        out_shape=jax.ShapeDtypeStruct((groups, 2, depth, width), jnp.bfloat16),
        compiler_params=pltpu.CompilerParams(vmem_limit_bytes=32 * 2**20),
        cost_estimate=pl.CostEstimate(
            flops=z_rows.size * groups * width,
            bytes_accessed=z_rows.size + 5 * own.size,
            transcendentals=0,
        ),
    )(z_rows, own, other)


def dot_part_kernel(core, z_ref, part_ref, *refs):
    out_ref = refs[-1]
    groups, _, depth, width = part_ref.shape
    first = (1 - lax.axis_index("zh")) * 8 + (lax.axis_index("c") ^ core) * 2
    for s in range(2):
        total = None if core == 0 else refs[0][s]
        for n in range(4):
            right = jnp.concatenate([part_ref[j, n] for j in range(groups)], axis=1)
            rows = z_ref[first + n // 2 * 4 + n % 2, s * depth : (s + 1) * depth, :]
            term = jnp.dot(rows, right, preferred_element_type=jnp.float32)
            total = term if total is None else total + term
        if core == 0:
            out_ref[s] = total
        else:
            for j in range(groups):
                out_ref[j, s] = total[:, j * width : (j + 1) * width].astype(out_ref.dtype)


def dot_part(core, z_rows, part, *sums):
    groups, _, depth, width = part.shape
    if core == 0:
        out = jax.ShapeDtypeStruct((2, depth, groups * width), jnp.float32)
    else:
        out = jax.ShapeDtypeStruct((groups, 2, depth, width), jnp.bfloat16)
    return pl.pallas_call(
        functools.partial(dot_part_kernel, core),
        in_specs=[pl.BlockSpec(memory_space=pltpu.VMEM)] * (2 + len(sums)),
        out_specs=pl.BlockSpec(memory_space=pltpu.VMEM),
        out_shape=out,
        compiler_params=pltpu.CompilerParams(vmem_limit_bytes=32 * 2**20),
        cost_estimate=pl.CostEstimate(
            flops=z_rows.size * groups * width // 2,
            bytes_accessed=z_rows.size // 2 + 5 * part.size,
            transcendentals=0,
        ),
    )(z_rows, part, *sums)


def other_core(block):
    return lax.ppermute(block, "c", SWAP)


def make_ident(shape, first_col):
    at = lax.axis_index
    rows = shape[1]
    row_ids = (
        lax.broadcasted_iota(jnp.int32, shape, 0) * 2048
        + at("y") // 2 * 1024
        + at("c") * 512
        + at("y") % 2 * rows
        + lax.broadcasted_iota(jnp.int32, shape, 1)
    )
    col_ids = first_col + lax.broadcasted_iota(jnp.int32, shape, 2)
    return jnp.where(row_ids == col_ids, 1.5, 0.0).astype(jnp.float32)


def make_shift(product, order, ident):
    poly = lax.reduce_precision(ident - 0.5 / order * product, 8, 7)
    return (poly - ident).astype(jnp.bfloat16)


def shards(z_iter, y_iter):
    at = lax.axis_index
    order = z_iter.shape[1] * lax.axis_size("x") * lax.axis_size("zl")
    z_half = z_iter.astype(jnp.bfloat16)
    y_half = y_iter.astype(jnp.bfloat16)
    z_rows = lax.all_gather(z_half, AXES, axis_index_groups=Z_RINGS)

    zh = at("zh")
    low = zh == 0
    first_col = at("x") * 2048 + at("zl") * 256 + zh * 128
    left, right = y_half[:, :128], y_half[:, 128:]
    mine = jnp.where(low, left, right)
    yours = lax.ppermute(jnp.where(low, right, left), "zh", SWAP)
    y_both = jnp.stack([jnp.where(low, mine, yours), jnp.where(low, yours, mine)])
    y_both = y_both.reshape(4, 256, 128)

    turn = [(i * 4 + j, j * 4 + i) for i in range(4) for j in range(4)]
    turned = lax.ppermute(y_both, PLANE, turn)
    y_own = lax.all_to_all(jnp.stack([turned] * 4), "y", 0, 0, tiled=True)
    y_other = other_core(y_own)
    y_other, ident = lax.optimization_barrier((y_other, make_ident((4, 256, 128), first_col)))
    part = dot_right_all(z_rows, y_own, y_other)

    part = lax.all_to_all(part.reshape(16, 256, 128), PLANE, 0, 0, tiled=True)
    product = part.reshape(4, 4, 256, 128).astype(jnp.float32).sum(0)
    shift = make_shift(product, order, ident)

    spread = jnp.broadcast_to(shift[:, None], (4, 4, 256, 128)).reshape(16, 256, 128)
    own = lax.all_to_all(spread, PLANE, 0, 0, tiled=True).reshape(4, 4, 256, 128)
    other = other_core(own)

    def sum_x(part):
        part = lax.all_to_all(part, "x", 0, 0, tiled=True)
        return part.astype(jnp.float32).sum(0).reshape(512, 128)

    yours = dot_part(1, z_rows, other, dot_part(0, z_rows, own))
    yours = sum_x(yours).astype(jnp.bfloat16)
    mine = dot_right(0, z_rows, own, other)
    yours = lax.ppermute(yours, "zh", SWAP).astype(jnp.float32)
    mine = lax.cond(
        at("c") < 2, sum_x, lambda part: jnp.zeros((512, 128), jnp.float32), mine
    )
    part = jnp.concatenate([jnp.where(low, mine, yours), jnp.where(low, yours, mine)], axis=1)
    return 1.5 * lax.reduce_precision(z_iter, 8, 7) + part


def solution(mesh):
    fine = Mesh(mesh.devices.reshape(SIZES), AXES)
    spec = P(("y", "zh", "c"), ("x", "zl"))
    return jax.shard_map(
        shards,
        mesh=fine,
        in_specs=(spec, spec),
        out_specs=spec,
        check_vma=False,
    )
```

```python
import functools

import jax
import jax.numpy as jnp
from jax import lax
from jax.experimental import pallas as pl
from jax.experimental.pallas import tpu as pltpu
from jax.sharding import Mesh
from jax.sharding import PartitionSpec as P

AXES = ("x", "zl", "y", "zh", "c")
SIZES = (4, 8, 4, 2, 2)
PLANE = ("x", "y")
SWAP = [(0, 1), (1, 0)]


def flat_id(x, zl, y, zh, c):
    return (((x * 8 + zl) * 4 + y) * 2 + zh) * 2 + c


Z_RINGS = [
    [flat_id(x, z % 8, y, z // 8, c) for z in range(16)]
    for x in range(4)
    for y in range(4)
    for c in range(2)
]


def dot_kernel(flips, z_ref, own_ref, other_ref, out_ref):
    groups, _, depth, width = own_ref.shape
    c = lax.axis_index("c")
    first = (lax.axis_index("zh") ^ flips) * 8
    for s in range(2):
        total = None
        for n in range(8):
            part = (own_ref, other_ref)[n // 4]
            right = jnp.concatenate([part[j, n % 4] for j in range(groups)], axis=1)
            chunk = first + (n % 4) // 2 * 4 + (c ^ (n // 4)) * 2 + n % 2
            rows = z_ref[chunk, s * depth : (s + 1) * depth, :]
            term = jnp.dot(rows, right, preferred_element_type=jnp.float32)
            total = term if total is None else total + term
        for j in range(groups):
            out_ref[j, s] = total[:, j * width : (j + 1) * width].astype(out_ref.dtype)


def dot_all_kernel(z_ref, right_ref, out_ref, left, sem):
    groups, _, depth, width = out_ref.shape
    copies = [pltpu.make_async_copy(z_ref.at[n], left.at[n], sem.at[n]) for n in range(16)]
    for copy in copies:
        copy.start()
    for zh in range(2):
        total = None
        for k in range(8):
            copies[zh * 8 + k].wait()
            term = jnp.dot(left[zh * 8 + k], right_ref[k], preferred_element_type=jnp.float32)
            total = term if total is None else total + term
        total = total.astype(out_ref.dtype)
        for s in range(2):
            for j in range(groups):
                block = total[s * depth : (s + 1) * depth, j * width : (j + 1) * width]
                out_ref[j, zh * 2 + s] = block


def dot_right_all(z_rows, own, other):
    groups, steps, depth, width = own.shape
    first = lax.axis_index("c") == 0
    right = jnp.stack([jnp.where(first, own, other), jnp.where(first, other, own)])
    right = right.reshape(2, groups, 2, 2, depth, width).transpose(2, 0, 3, 4, 1, 5)
    right = right.reshape(8, depth, groups * width)
    return pl.pallas_call(
        dot_all_kernel,
        in_specs=[pl.BlockSpec(memory_space=pl.ANY), pl.BlockSpec(memory_space=pltpu.VMEM)],
        out_specs=pl.BlockSpec(memory_space=pltpu.VMEM),
        out_shape=jax.ShapeDtypeStruct(own.shape, jnp.bfloat16),
        scratch_shapes=[
            pltpu.VMEM(z_rows.shape, jnp.bfloat16),
            pltpu.SemaphoreType.DMA((16,)),
        ],
        compiler_params=pltpu.CompilerParams(vmem_limit_bytes=48 * 2**20),
        cost_estimate=pl.CostEstimate(
            flops=2 * z_rows.size * groups * width,
            bytes_accessed=2 * (z_rows.size + 3 * own.size),
            transcendentals=0,
        ),
    )(z_rows, right)


def dot_right(flips, z_rows, own, other):
    groups, steps, depth, width = own.shape
    return pl.pallas_call(
        functools.partial(dot_kernel, flips),
        in_specs=[pl.BlockSpec(memory_space=pltpu.VMEM)] * 3,
        out_specs=pl.BlockSpec(memory_space=pltpu.VMEM),
        out_shape=jax.ShapeDtypeStruct((groups, 2, depth, width), jnp.bfloat16),
        compiler_params=pltpu.CompilerParams(vmem_limit_bytes=32 * 2**20),
        cost_estimate=pl.CostEstimate(
            flops=z_rows.size * groups * width,
            bytes_accessed=z_rows.size + 5 * own.size,
            transcendentals=0,
        ),
    )(z_rows, own, other)


def dot_part_kernel(core, z_ref, part_ref, *refs):
    out_ref = refs[-1]
    groups, _, depth, width = part_ref.shape
    first = (1 - lax.axis_index("zh")) * 8 + (lax.axis_index("c") ^ core) * 2
    for s in range(2):
        total = None if core == 0 else refs[0][s]
        for n in range(4):
            right = jnp.concatenate([part_ref[j, n] for j in range(groups)], axis=1)
            rows = z_ref[first + n // 2 * 4 + n % 2, s * depth : (s + 1) * depth, :]
            term = jnp.dot(rows, right, preferred_element_type=jnp.float32)
            total = term if total is None else total + term
        if core == 0:
            out_ref[s] = total
        else:
            for j in range(groups):
                out_ref[j, s] = total[:, j * width : (j + 1) * width].astype(out_ref.dtype)


def dot_part(core, z_rows, part, *sums):
    groups, _, depth, width = part.shape
    if core == 0:
        out = jax.ShapeDtypeStruct((2, depth, groups * width), jnp.float32)
    else:
        out = jax.ShapeDtypeStruct((groups, 2, depth, width), jnp.bfloat16)
    return pl.pallas_call(
        functools.partial(dot_part_kernel, core),
        in_specs=[pl.BlockSpec(memory_space=pltpu.VMEM)] * (2 + len(sums)),
        out_specs=pl.BlockSpec(memory_space=pltpu.VMEM),
        out_shape=out,
        compiler_params=pltpu.CompilerParams(vmem_limit_bytes=32 * 2**20),
        cost_estimate=pl.CostEstimate(
            flops=z_rows.size * groups * width // 2,
            bytes_accessed=z_rows.size // 2 + 5 * part.size,
            transcendentals=0,
        ),
    )(z_rows, part, *sums)


def other_core(block):
    return lax.ppermute(block, "c", SWAP)


def make_ident(shape, first_col):
    at = lax.axis_index
    rows = shape[1]
    row_ids = (
        lax.broadcasted_iota(jnp.int32, shape, 0) * 2048
        + at("y") // 2 * 1024
        + at("c") * 512
        + at("y") % 2 * rows
        + lax.broadcasted_iota(jnp.int32, shape, 1)
    )
    col_ids = first_col + lax.broadcasted_iota(jnp.int32, shape, 2)
    return jnp.where(row_ids == col_ids, 1.5, 0.0).astype(jnp.float32)


def make_shift(product, order, ident):
    poly = lax.reduce_precision(ident - 0.5 / order * product, 8, 7)
    return (poly - ident).astype(jnp.bfloat16)


def shards(z_iter, y_iter):
    at = lax.axis_index
    order = z_iter.shape[1] * lax.axis_size("x") * lax.axis_size("zl")
    z_half = z_iter.astype(jnp.bfloat16)
    y_half = y_iter.astype(jnp.bfloat16)
    z_rows = lax.all_gather(z_half, AXES, axis_index_groups=Z_RINGS)

    zh = at("zh")
    low = zh == 0
    first_col = at("x") * 2048 + at("zl") * 256 + zh * 128
    left, right = y_half[:, :128], y_half[:, 128:]
    mine = jnp.where(low, left, right)
    yours = lax.ppermute(jnp.where(low, right, left), "zh", SWAP)
    y_both = jnp.stack([jnp.where(low, mine, yours), jnp.where(low, yours, mine)])
    y_both = y_both.reshape(4, 256, 128)

    turn = [(i * 4 + j, j * 4 + i) for i in range(4) for j in range(4)]
    turned = lax.ppermute(y_both, PLANE, turn)
    y_own = lax.all_to_all(jnp.stack([turned] * 4), "y", 0, 0, tiled=True)
    y_other = other_core(y_own)
    y_other, ident = lax.optimization_barrier((y_other, make_ident((4, 256, 128), first_col)))
    part = dot_right_all(z_rows, y_own, y_other)

    part = lax.all_to_all(part.reshape(16, 256, 128), PLANE, 0, 0, tiled=True)
    product = part.reshape(4, 4, 256, 128).astype(jnp.float32).sum(0)
    shift = make_shift(product, order, ident)

    spread = jnp.broadcast_to(shift[:, None], (4, 4, 256, 128)).reshape(16, 256, 128)
    own = lax.all_to_all(spread, PLANE, 0, 0, tiled=True).reshape(4, 4, 256, 128)
    other = other_core(own)

    def sum_x(part):
        part = lax.all_to_all(part, "x", 0, 0, tiled=True)
        return part.astype(jnp.float32).sum(0).reshape(512, 128)

    yours = dot_part(1, z_rows, other, dot_part(0, z_rows, own))
    yours = sum_x(yours).astype(jnp.bfloat16)
    mine = dot_right(0, z_rows, own, other)
    yours = lax.ppermute(yours, "zh", SWAP)
    mine = lax.cond(
        at("c") < 2, sum_x, lambda part: jnp.zeros((512, 128), jnp.float32), mine
    )
    z_part = 1.5 * lax.reduce_precision(z_iter, 8, 7)
    mine += jnp.where(low, z_part[:, :128], z_part[:, 128:])
    yours, mine = lax.optimization_barrier((yours, mine))
    yours = yours.astype(jnp.float32) + jnp.where(low, z_part[:, 128:], z_part[:, :128])
    return jnp.concatenate([jnp.where(low, mine, yours), jnp.where(low, yours, mine)], axis=1)


def solution(mesh):
    fine = Mesh(mesh.devices.reshape(SIZES), AXES)
    spec = P(("y", "zh", "c"), ("x", "zl"))
    return jax.shard_map(
        shards,
        mesh=fine,
        in_specs=(spec, spec),
        out_specs=spec,
        check_vma=False,
    )
```
